32 devices in a mesh: rep: 2 (over x), dp: 2 (over y), seq: 8 (over z, core).
Axes of the slice: x: 2, y: 2, z: 4, core: 2. Of those that a mesh axis runs over, the one named last changes fastest.
Arguments:
- tokens: bfloat16 [4, 16, 8, 16, 768], P(('rep', 'dp'), 'seq'), may hold values from -6 to 6
- cotangent: bfloat16 [4, 16, 8, 16, 768], P(('rep', 'dp'), 'seq'), may hold values from -6 to 6
- w_qkv: bfloat16 [768, 2304], P('dp'), may hold values from -0.21875 to 0.21875
- w_proj: bfloat16 [768, 768], P('dp'), may hold values from -0.21875 to 0.21875
- conv_weight: float32 [27, 768], replicated, may hold values from -1.25 to 1.25
- norm_gain: float32 [768], replicated, may hold values from 0.5 to 1.5
- head_scale: float32 [24], replicated, may hold values from 2 to 20
- shift_offsets: int32 [2], replicated, may hold values from 1 to 7, as said below
Outputs:
- output: bfloat16 [4, 16, 8, 16, 768], P(('rep', 'dp'), 'seq')
- grad_tokens: bfloat16 [4, 16, 8, 16, 768], P(('rep', 'dp'), 'seq')
- grad_qkv: float32 [768, 2304], P('dp')
- grad_proj: float32 [768, 768], P('dp')
- grad_conv: float32 [27, 768], replicated
- grad_gain: float32 [768], replicated
- grad_scale: float32 [24], replicated
The draws below stay inside these ranges and needn't reach their ends.
Inputs may be any that keep to these rules, and one draw needn't show every extreme that they name: `shift_offsets`: the two offsets differ.
All inputs are finite; a program needn't handle non-finite values.
Results may differ from the reference program's by a relative error of at most 0.014.
The reference program's roundings to bfloat16 on the way count: a program that leaves them out, or rounds other values in their place, can miss the bound.
Values may be sent and summed in bfloat16 or wider, within the bound.
No kernel may reach another device: no remote copies, remote signals or barrier semaphores. Data moves between devices by JAX's collectives and lax.ppermute only.
A program may use at most 128 MiB of HBM per device.

```python
import math
import jax
import jax.numpy as jnp
from jax import lax

C = 768
HEADS = 24
WD = 4
WH = 8
WW = 8
DL = 2
HH = 8
WIDE = 16
DEPTH = 16
GROUPS = 4


def draw_shift_offsets(key, part):
    largest = min(WH, WW) - 1
    which = jax.random.randint(jax.random.fold_in(key, 11), (), 0, 2)
    other = jax.random.randint(jax.random.fold_in(key, 12), (), 1, largest)
    top = jnp.array(largest, jnp.int32)
    first = jnp.where(which == 0, top, other.astype(jnp.int32))
    second = jnp.where(which == 0, other.astype(jnp.int32), top)
    return jnp.stack([first, second]).astype(jnp.int32)


def block_scale(own_key, extent, shards, low, high):
    def one(position, shards_of):
        draws = jax.random.uniform(jax.random.fold_in(jax.random.fold_in(own_key, 6), position), (shards_of,), jnp.float32, low / len(shards), high / len(shards))
        return jnp.repeat(jnp.exp(draws), extent[position] // shards_of).reshape((-1,) + (1,) * (len(extent) - position - 1))

    loudness = one(*shards[0])
    for cut in shards[1:]:
        loudness = loudness * one(*cut)
    return loudness


def scatter_about(key, dims, scale, bound, shards=(), dtype=jnp.bfloat16):
    values = scale * jax.random.normal(key, dims, jnp.float32)
    if shards:
        values = values * block_scale(key, dims, shards, -0.22, 0.18)
    return jnp.clip(values, -bound, bound).astype(dtype)


def setup_inputs(seed: int = 0) -> dict:
    splits = jax.random.split(jax.random.key(seed), 9)
    return {
        "tokens": scatter_about(splits[0], (GROUPS, DEPTH, HH, WIDE, C), 1.0, 6.0, ((0, 4), (1, 8))),
        "cotangent": scatter_about(splits[1], (GROUPS, DEPTH, HH, WIDE, C), 1.0, 6.0, ((0, 4), (1, 8))),
        "w_qkv": scatter_about(splits[2], (C, 3 * C), C ** -0.5, 0.21875, ((0, 2),)),
        "w_proj": scatter_about(splits[3], (C, C), C ** -0.5, 0.21875, ((0, 2),)),
        "conv_weight": scatter_about(splits[4], (27, C), 27 ** -0.5, 1.25, (), jnp.float32),
        "norm_gain": jnp.clip(1.0 + 0.1 * jax.random.normal(splits[5], (C,), jnp.float32), 0.5, 1.5),
        "head_scale": jnp.clip(jnp.exp(jax.random.uniform(splits[6], (HEADS,), jnp.float32, math.log(2.0), math.log(20.0))), 2.0, 20.0),
        "shift_offsets": draw_shift_offsets(jax.random.fold_in(splits[8], 71), 0),
    }


def tap_sum(padded, weight, slab_depth, height, grid_width, flipped):
    summed = jnp.zeros((slab_depth, height, grid_width, padded.shape[-1]), jnp.float32)
    for depth_tap in range(3):
        for row_tap in range(3):
            for col_tap in range(3):
                tap_index = 9 * depth_tap + 3 * row_tap + col_tap
                if flipped:
                    starts = (2 - depth_tap, 2 - row_tap, 2 - col_tap)
                else:
                    starts = (depth_tap, row_tap, col_tap)
                window_part = padded[starts[0]:starts[0] + slab_depth, starts[1]:starts[1] + height, starts[2]:starts[2] + grid_width]
                summed = summed + weight[tap_index] * window_part.astype(jnp.float32)
    return summed

def into_windows(field):
    slab_depth, height, grid_width, channels = field.shape
    shaped = field.reshape(slab_depth // WD, WD, height // WH, WH, grid_width // WW, WW, channels)
    shaped = shaped.transpose(0, 2, 4, 1, 3, 5, 6)
    return shaped.reshape(slab_depth // WD, height // WH * (grid_width // WW), WD * WH * WW, channels)

def out_of_windows(blocks, slab_depth, height, grid_width):
    channels = blocks.shape[-1]
    shaped = blocks.reshape(slab_depth // WD, height // WH, grid_width // WW, WD, WH, WW, channels)
    shaped = shaped.transpose(0, 3, 1, 4, 2, 5, 6)
    return shaped.reshape(slab_depth, height, grid_width, channels)

def unit_rows(values):
    as_float = values.astype(jnp.float32)
    radius = jnp.sqrt(lax.optimization_barrier(jnp.sum(as_float * as_float, axis=-1, keepdims=True)) + 1.0)
    return (as_float, radius, (as_float / radius).astype(jnp.bfloat16))

def radius_back(as_float, radius, back_unit):
    inner = lax.optimization_barrier(jnp.sum(as_float * back_unit, axis=-1, keepdims=True))
    return back_unit / radius - as_float * inner / (radius * radius * radius)

def window_forward(unit_query, unit_key, values, allowed, head_scale):
    cosine = jnp.einsum('wqhe,wkhe->whqk', unit_query.astype(jnp.float32), unit_key.astype(jnp.float32))
    expo = jnp.exp(head_scale[:, None, None] * cosine) * allowed[:, None]
    probability = expo / lax.optimization_barrier(jnp.sum(expo, axis=-1, keepdims=True))
    weights = probability.astype(jnp.bfloat16)
    attended = jnp.einsum('whqk,wkhe->wqhe', weights.astype(jnp.float32), values.astype(jnp.float32)).astype(jnp.bfloat16)
    return (cosine, probability, weights, attended)

def window_backward(unit_query, unit_key, values, allowed, head_scale, back_attended):
    cosine, probability, weights, unused = window_forward(unit_query, unit_key, values, allowed, head_scale)
    back_float = back_attended.astype(jnp.float32)
    back_value = jnp.einsum('whqk,wqhe->wkhe', weights.astype(jnp.float32), back_float)
    back_prob = jnp.einsum('wqhe,wkhe->whqk', back_float, values.astype(jnp.float32))
    back_score = probability * (back_prob - lax.optimization_barrier(jnp.sum(probability * back_prob, axis=-1, keepdims=True)))
    scale_rows = lax.optimization_barrier(jnp.sum(back_score * cosine, axis=-1))
    scaled = (back_score * head_scale[:, None, None]).astype(jnp.bfloat16)
    back_uq = jnp.einsum('whqk,wkhe->wqhe', scaled.astype(jnp.float32), unit_key.astype(jnp.float32))
    back_uk = jnp.einsum('whqk,wqhe->wkhe', scaled.astype(jnp.float32), unit_query.astype(jnp.float32))
    return (back_uq, back_uk, back_value, scale_rows)

def one_group(tokens, cotangent, w_qkv, w_proj, conv_weight, norm_gain, head_scale, shift_offsets):
    slab_depth, height, grid_width, channels = tokens.shape
    head_count = head_scale.shape[0]
    head_dim = channels // head_count
    rows_shift = shift_offsets[0]
    cols_shift = shift_offsets[1]
    spatial = ((1, 1), (1, 1), (1, 1), (0, 0))
    padded_tokens = jnp.pad(tokens, spatial)
    mixed_field = tokens.astype(jnp.float32) + tap_sum(padded_tokens, conv_weight, slab_depth, height, grid_width, False)
    centred = mixed_field - lax.optimization_barrier(jnp.mean(mixed_field, axis=-1, keepdims=True))
    inverse_std = lax.rsqrt(lax.optimization_barrier(jnp.mean(centred * centred, axis=-1, keepdims=True)) + 1e-05)
    unit_field = centred * inverse_std
    normed = (unit_field * norm_gain).astype(jnp.bfloat16)
    shifted = jnp.roll(normed, (-DL, -rows_shift, -cols_shift), axis=(0, 1, 2))
    position_count = slab_depth * height * grid_width
    shifted_rows = shifted.reshape(position_count, channels)
    qkv = jnp.dot(shifted_rows, w_qkv, preferred_element_type=jnp.float32).astype(jnp.bfloat16)
    qkv_windows = into_windows(qkv.reshape(slab_depth, height, grid_width, 3 * channels))
    row_code = 2 * (jnp.arange(height) >= height - rows_shift).astype(jnp.int32)
    col_code = (jnp.arange(grid_width) >= grid_width - cols_shift).astype(jnp.int32)
    grid_code = jnp.broadcast_to((row_code[:, None] + col_code[None, :])[None], (slab_depth, height, grid_width))
    code_windows = into_windows(grid_code[..., None])[..., 0]
    block_count = qkv_windows.shape[1]
    positions = qkv_windows.shape[2]

    def split_heads(part):
        return part.reshape(block_count, positions, head_count, head_dim)

    def prepare(qkv_block, code_block):
        allowed = (code_block[:, :, None] == code_block[:, None, :]).astype(jnp.float32)
        query = split_heads(qkv_block[..., :channels])
        key_part = split_heads(qkv_block[..., channels:2 * channels])
        value_part = split_heads(qkv_block[..., 2 * channels:])
        return (allowed, query, key_part, value_part)

    def forward_block(packed):
        allowed, query, key_part, value_part = prepare(packed[0], packed[1])
        unused_a, unused_b, unit_query = unit_rows(query)
        unused_c, unused_d, unit_key = unit_rows(key_part)
        return window_forward(unit_query, unit_key, value_part, allowed, head_scale)[3]
    attended = lax.map(forward_block, (qkv_windows, code_windows))
    attended = attended.reshape(attended.shape[0], block_count, positions, channels)
    restored = jnp.roll(out_of_windows(attended, slab_depth, height, grid_width), (DL, rows_shift, cols_shift), axis=(0, 1, 2))
    restored_rows = restored.reshape(position_count, channels)
    projected = jnp.dot(restored_rows, w_proj, preferred_element_type=jnp.float32)
    output = (mixed_field + projected.reshape(slab_depth, height, grid_width, channels)).astype(jnp.bfloat16)
    cotangent_rows = cotangent.reshape(position_count, channels)
    back_restored = jnp.dot(cotangent_rows, w_proj.T, preferred_element_type=jnp.float32).astype(jnp.bfloat16)
    back_attended = jnp.roll(back_restored.reshape(slab_depth, height, grid_width, channels), (-DL, -rows_shift, -cols_shift), axis=(0, 1, 2))
    back_windows = into_windows(back_attended)

    def backward_block(packed):
        allowed, query, key_part, value_part = prepare(packed[0], packed[1])
        query_float, query_radius, unit_query = unit_rows(query)
        key_float, key_radius, unit_key = unit_rows(key_part)
        back_heads = split_heads(packed[2])
        back_uq, back_uk, back_value, scale_rows = window_backward(unit_query, unit_key, value_part, allowed, head_scale, back_heads)
        back_query = radius_back(query_float, query_radius, back_uq)
        back_key = radius_back(key_float, key_radius, back_uk)
        joined = jnp.concatenate([back_query.reshape(block_count, positions, channels), back_key.reshape(block_count, positions, channels), back_value.reshape(block_count, positions, channels)], axis=-1)
        return (joined.astype(jnp.bfloat16), lax.optimization_barrier(jnp.sum(scale_rows, axis=(0, 2))))
    back_qkv_windows, scale_parts = lax.map(backward_block, (qkv_windows, code_windows, back_windows))
    back_qkv = out_of_windows(back_qkv_windows, slab_depth, height, grid_width)
    back_qkv_rows = back_qkv.reshape(position_count, 3 * channels)
    qkv_part = jnp.dot(shifted_rows.T, back_qkv_rows, preferred_element_type=jnp.float32)
    proj_part = jnp.dot(restored_rows.T, cotangent_rows, preferred_element_type=jnp.float32)
    back_shifted = jnp.dot(back_qkv_rows, w_qkv.T, preferred_element_type=jnp.float32).astype(jnp.bfloat16)
    back_normed = jnp.roll(back_shifted.reshape(slab_depth, height, grid_width, channels), (DL, rows_shift, cols_shift), axis=(0, 1, 2))
    back_float = back_normed.astype(jnp.float32)
    gain_part = lax.optimization_barrier(jnp.sum(back_float * unit_field, axis=(0, 1, 2)))
    grad_unit = back_float * norm_gain
    back_mixed = cotangent.astype(jnp.float32) + inverse_std * (grad_unit - lax.optimization_barrier(jnp.mean(grad_unit, axis=-1, keepdims=True)) - unit_field * lax.optimization_barrier(jnp.mean(grad_unit * unit_field, axis=-1, keepdims=True)))
    padded_back = jnp.pad(back_mixed, spatial)
    grad_tokens = (back_mixed + tap_sum(padded_back, conv_weight, slab_depth, height, grid_width, True)).astype(jnp.bfloat16)
    conv_rows = []
    for depth_tap in range(3):
        for row_tap in range(3):
            for col_tap in range(3):
                window_part = padded_tokens[depth_tap:depth_tap + slab_depth, row_tap:row_tap + height, col_tap:col_tap + grid_width]
                conv_rows.append(lax.optimization_barrier(jnp.sum(back_mixed * window_part.astype(jnp.float32), axis=(0, 1, 2))))
    conv_part = jnp.stack(conv_rows)
    return (output, grad_tokens, qkv_part, proj_part, conv_part, gain_part, lax.optimization_barrier(jnp.sum(scale_parts, axis=0)))

def reference(tokens, cotangent, w_qkv, w_proj, conv_weight, norm_gain, head_scale, shift_offsets):

    def per_group(packed):
        return one_group(packed[0], packed[1], w_qkv, w_proj, conv_weight, norm_gain, head_scale, shift_offsets)
    results = lax.map(per_group, (tokens, cotangent))
    factor = 1.0 / math.sqrt(GROUPS * DEPTH * HH * WIDE)
    return (results[0], results[1], lax.optimization_barrier(jnp.sum(results[2], axis=0)) * factor, lax.optimization_barrier(jnp.sum(results[3], axis=0)) * factor, lax.optimization_barrier(jnp.sum(results[4], axis=0)) * factor, lax.optimization_barrier(jnp.sum(results[5], axis=0)) * factor, lax.optimization_barrier(jnp.sum(results[6], axis=0)) * factor)
```

```python
import functools
import math

import jax
import jax.numpy as jnp
from jax import lax
from jax.experimental import pallas as pl
from jax.experimental.pallas import tpu as pltpu
from jax.sharding import PartitionSpec as P

HALF = 8
BF = jnp.bfloat16
F32 = jnp.float32


def swapped(x, axis, flip):
    count = 1
    for name in (axis,) if isinstance(axis, str) else axis:
        count = count * lax.axis_size(name)
    return lax.ppermute(x, axis, [(i, i ^ flip) for i in range(count)])


def window_partner(x):
    count = lax.axis_size("seq")
    pairs = [(i, (i + 1) % count if i % 2 else (i - 1) % count) for i in range(count)]
    return lax.ppermute(x, "seq", pairs)


def with_halo(x):
    count = lax.axis_size("seq")
    up = [(i, i + 1) for i in range(count - 1)]
    down = [(j, i) for i, j in up]
    before = lax.ppermute(x[-1:], "seq", up)
    after = lax.ppermute(x[:1], "seq", down)
    return jnp.concatenate([before, x, after], axis=0)


def tap_sum(padded, weight, slab_depth, height, grid_width, flipped):
    summed = jnp.zeros((slab_depth, height, grid_width, padded.shape[-1]), F32)
    for a in range(3):
        for b in range(3):
            for e in range(3):
                starts = (2 - a, 2 - b, 2 - e) if flipped else (a, b, e)
                part = padded[
                    starts[0] : starts[0] + slab_depth,
                    starts[1] : starts[1] + height,
                    starts[2] : starts[2] + grid_width,
                ]
                summed = summed + weight[9 * a + 3 * b + e] * part.astype(F32)
    return summed


def attention_kernel(head_dim, head_count, nums, scale, qkv, ba, att, back, gs):
    n = qkv.shape[1]
    channels = head_count * head_dim
    rows_shift, cols_shift, second = nums[0], nums[1], nums[2]

    def code(dim):
        t = lax.broadcasted_iota(jnp.int32, (n, n), dim)
        row = (t >> 3) & 7
        col = t & 7
        first_bit = jnp.where(row < rows_shift, 2, 0)
        return first_bit + jnp.where(col < cols_shift, second, 0)

    allowed = jnp.where(code(0) == code(1), 1.0, 0.0).astype(F32)
    over_rows = (((0,), (0,)), ((), ()))
    over_lanes = (((1,), (1,)), ((), ()))

    def unit(raw):
        inverse = lax.rsqrt(jnp.sum(raw * raw, axis=0, keepdims=True) + 1.0)
        return inverse, (raw * inverse).astype(BF)

    def radius_back(raw, inverse, grad):
        inner = jnp.sum(raw * grad, axis=0, keepdims=True)
        return grad * inverse - raw * (inner * (inverse * inverse * inverse))

    def one_head(h):
        def rows(base):
            return pl.ds(pl.multiple_of(base + h * head_dim, head_dim), head_dim)

        s = scale[h]
        qf = qkv[rows(0), :].astype(F32)
        kf = qkv[rows(channels), :].astype(F32)
        v = qkv[rows(2 * channels), :]
        b = ba[rows(0), :]
        iq, uq = unit(qf)
        ik, uk = unit(kf)
        cosine = lax.dot_general(uk, uq, over_rows, preferred_element_type=F32)
        expo = jnp.exp(cosine * s) * allowed
        prob = expo * (1.0 / jnp.sum(expo, axis=0, keepdims=True))
        weights = prob.astype(BF)
        att[rows(0), :] = jnp.dot(v, weights, preferred_element_type=F32).astype(BF)
        back_prob = lax.dot_general(v, b, over_rows, preferred_element_type=F32)
        mean = jnp.sum(prob * back_prob, axis=0, keepdims=True)
        back_score = prob * (back_prob - mean)
        gs[pl.ds(h, 1), :] = jnp.sum(back_score * cosine, axis=0, keepdims=True)
        scaled = (back_score * s).astype(BF)
        buq = jnp.dot(uk, scaled, preferred_element_type=F32)
        buk = lax.dot_general(uq, scaled, over_lanes, preferred_element_type=F32)
        bv = lax.dot_general(b, weights, over_lanes, preferred_element_type=F32)
        back[rows(0), :] = radius_back(qf, iq, buq).astype(BF)
        back[rows(channels), :] = radius_back(kf, ik, buk).astype(BF)
        back[rows(2 * channels), :] = bv.astype(BF)

    def body(i, carry):
        for u in range(4):
            one_head(i * 4 + u)
        return carry

    lax.fori_loop(0, head_count // 4, body, 0)


def window_attention(nums, scale, qkv, ba):
    head_count = scale.shape[0]
    channels, n = ba.shape
    vmem = pl.BlockSpec(memory_space=pltpu.VMEM)
    smem = pl.BlockSpec(memory_space=pltpu.SMEM)
    return pl.pallas_call(
        functools.partial(attention_kernel, channels // head_count, head_count),
        out_shape=(
            jax.ShapeDtypeStruct((channels, n), BF),
            jax.ShapeDtypeStruct((3 * channels, n), BF),
            jax.ShapeDtypeStruct((head_count, n), F32),
        ),
        in_specs=[smem, smem, vmem, vmem],
        out_specs=(vmem, vmem, vmem),
        compiler_params=pltpu.CompilerParams(vmem_limit_bytes=32 * 1024 * 1024),
        cost_estimate=pl.CostEstimate(
            flops=14 * n * n * channels,
            bytes_accessed=16 * n * channels,
            transcendentals=n * n * head_count,
        ),
        name="window_attention",
    )(nums, scale, qkv, ba)


def pick(x, index, axis):
    return lax.dynamic_index_in_dim(x, index, axis, keepdims=False)


def tree_sum(parts):
    while len(parts) > 1:
        parts = [a + b for a, b in zip(parts[::2], parts[1::2])]
    return parts[0]


def chip_stages(chips):
    stages = []
    left = chips
    while left > 1:
        radix = 4 if left % 4 == 0 else 2
        left = left // radix
        stages.append((radix, left))
    return stages


def scatter_sum(grad, where):
    rep, dp, chip, core, chips = where
    rows = grad.shape[0] // (8 * chips)
    parts = grad.reshape(2, 2, chips, 2, rows, grad.shape[1])
    other = swapped(pick(parts, 1 - core, 3).astype(BF), "seq", 1)
    total = pick(parts, core, 3) + other.astype(F32)
    got = []
    for k in range(4):
        block = pick(pick(total, dp ^ (k & 1), 0), rep ^ (k >> 1), 0)
        got.append(swapped(block.astype(BF), ("rep", "dp"), k).astype(F32) if k else block)
    total = tree_sum(got)
    for radix, stride in chip_stages(chips):
        digit = (chip // stride) % radix
        parts = total.reshape((radix, stride) + total.shape[1:])
        got = []
        for k in range(radix):
            block = pick(parts, digit ^ k, 0)
            got.append(swapped(block.astype(BF), "seq", 2 * k * stride).astype(F32) if k else block)
        total = tree_sum(got)
    return total[0]


def gather_rows(block, where):
    rep, dp, chip, core, chips = where
    held = block.astype(BF)[None]
    for radix, stride in chip_stages(chips)[::-1]:
        digit = (chip // stride) % radix
        got = [swapped(held, "seq", 2 * k * stride) if k else held for k in range(radix)]
        bunch = jnp.stack(got)
        held = jnp.concatenate([pick(bunch, digit ^ j, 0) for j in range(radix)])
    got = swapped(held, "rep", 1)
    held = jnp.stack([jnp.where(rep == 0, held, got), jnp.where(rep == 0, got, held)])
    got = swapped(held, "seq", 1)
    first = jnp.where(core == 0, held, got)
    second = jnp.where(core == 0, got, held)
    return jnp.stack([first, second], axis=2).reshape(-1, block.shape[1])


def sum_everywhere(x, where):
    chips = where[4]
    x = x + swapped(x, "seq", 1)
    x = tree_sum([swapped(x, ("rep", "dp"), k) if k else x for k in range(4)])
    for radix, stride in chip_stages(chips):
        x = tree_sum([swapped(x, "seq", 2 * k * stride) if k else x for k in range(radix)])
    return x


def full_weights(mine, dp, core):
    half = mine.shape[0] // 2
    part = lax.dynamic_slice_in_dim(mine, core * half, half, 0)
    got = swapped(part, "dp", 1)
    other = swapped(got, "seq", 1)
    m0, m1 = mine[:half], mine[half:]
    p0, p1 = jnp.where(core == 0, got, other), jnp.where(core == 0, other, got)
    low = dp == 0
    return jnp.concatenate(
        [jnp.where(low, a, b) for a, b in ((m0, p0), (m1, p1), (p0, m0), (p1, m1))]
    )


def per_device(tokens, cotangent, w_qkv, w_proj, conv_weight, norm_gain, head_scale, shift_offsets):
    slab = tokens[0]
    cot = cotangent[0]
    depth, height, width, channels = slab.shape
    head_count = head_scale.shape[0]
    seq_count = lax.axis_size("seq")
    seq_index = lax.axis_index("seq")
    core = seq_index % 2
    rep, dp = lax.axis_index("rep"), lax.axis_index("dp")
    where = (rep, dp, seq_index // 2, core, seq_count // 2)
    rows_shift, cols_shift = shift_offsets[0], shift_offsets[1]
    positions = depth * height * width
    half = positions // 2
    columns = jnp.arange(HALF)[None, None, :, None]
    straight = (columns >= cols_shift) == (core == 1)

    def split_columns(field):
        low, high = field[:, :, :HALF], field[:, :, HALF:]
        return (
            jnp.where(straight, low, high).reshape(half, -1),
            jnp.where(straight, high, low).reshape(half, -1),
        )

    def join_columns(mine, theirs):
        mine = mine.reshape(depth, height, HALF, -1)
        theirs = theirs.reshape(depth, height, HALF, -1)
        return jnp.concatenate(
            [jnp.where(straight, mine, theirs), jnp.where(straight, theirs, mine)], axis=2
        )

    weights = full_weights(jnp.concatenate([w_qkv, w_proj], axis=1), dp, core)
    full_qkv, full_proj = weights[:, : 3 * channels], weights[:, 3 * channels :]

    spatial = ((0, 0), (1, 1), (1, 1), (0, 0))
    padded_tokens = jnp.pad(with_halo(slab), spatial)
    cot_mine, cot_theirs = split_columns(cot)
    cot_window = jnp.concatenate([cot_mine, window_partner(cot_theirs)])
    mixed_field = slab.astype(F32) + tap_sum(
        padded_tokens, conv_weight, depth, height, width, False
    )
    centred = mixed_field - jnp.mean(mixed_field, axis=-1, keepdims=True)
    inverse_std = lax.rsqrt(jnp.mean(centred * centred, axis=-1, keepdims=True) + 1e-05)
    unit_field = centred * inverse_std
    normed = (unit_field * norm_gain).astype(BF)
    x_mine, x_theirs = split_columns(normed)
    x_window = jnp.concatenate([x_mine, window_partner(x_theirs)])

    qkv = jnp.einsum("tk,kc->ct", x_window, full_qkv, preferred_element_type=F32).astype(BF)
    back_attended = jnp.einsum(
        "td,cd->ct", cot_window, full_proj, preferred_element_type=F32
    ).astype(BF)
    nums = jnp.stack([rows_shift, cols_shift, 1 - core]).astype(jnp.int32)
    attended, back_qkv, scale_rows = window_attention(nums, head_scale, qkv, back_attended)

    proj_term = jnp.einsum("ct,td->cd", attended, cot_window, preferred_element_type=F32)
    qkv_term = jnp.einsum("tc,jt->cj", x_window, back_qkv, preferred_element_type=F32)
    back_shifted = jnp.einsum(
        "jt,cj->tc", back_qkv, full_qkv, preferred_element_type=F32
    ).astype(BF)
    back_normed = join_columns(back_shifted[:half], window_partner(back_shifted[half:]))

    grads = scatter_sum(jnp.concatenate([qkv_term, proj_term], axis=1), where)
    factor = 1.0 / math.sqrt(
        lax.axis_size("rep") * lax.axis_size("dp") * seq_count * positions
    )
    grads = gather_rows(grads, where).astype(F32) * factor

    att_theirs = window_partner(attended[:, half:])
    att_mine = attended[:, :half]
    lane_straight = ((jnp.arange(half) % HALF)[None, :] >= cols_shift) == (core == 1)
    projected = [
        jnp.einsum("ct,cd->td", side, full_proj, preferred_element_type=F32).reshape(
            depth, height, HALF, channels
        )
        for side in (
            jnp.where(lane_straight, att_mine, att_theirs),
            jnp.where(lane_straight, att_theirs, att_mine),
        )
    ]
    output = (mixed_field + jnp.concatenate(projected, axis=2)).astype(BF)

    back_float = back_normed.astype(F32)
    gain_part = jnp.sum(back_float * unit_field, axis=(0, 1, 2))
    grad_unit = back_float * norm_gain
    back_mixed = cot.astype(F32) + inverse_std * (
        grad_unit
        - jnp.mean(grad_unit, axis=-1, keepdims=True)
        - unit_field * jnp.mean(grad_unit * unit_field, axis=-1, keepdims=True)
    )
    padded_back = jnp.pad(with_halo(back_mixed.astype(BF)).astype(F32), spatial)
    grad_tokens = (
        back_mixed + tap_sum(padded_back, conv_weight, depth, height, width, True)
    ).astype(BF)
    conv_rows = []
    for a in range(3):
        for b in range(3):
            for e in range(3):
                part = padded_tokens[a : a + depth, b : b + height, e : e + width]
                conv_rows.append(jnp.sum(back_mixed * part.astype(F32), axis=(0, 1, 2)))
    scale_part = jnp.sum(scale_rows, axis=1)
    small = jnp.stack(conv_rows + [gain_part, jnp.pad(scale_part, (0, channels - head_count))])
    small = sum_everywhere(small, where) * factor
    taps = conv_weight.shape[0]
    return (
        output[None],
        grad_tokens[None],
        grads[:, : 3 * channels],
        grads[:, 3 * channels :],
        small[:taps],
        small[taps],
        small[taps + 1, :head_count],
    )


def solution(mesh):
    block = P(("rep", "dp"), "seq", None, None, None)
    rows = P("dp", None)
    return jax.shard_map(
        per_device,
        mesh=mesh,
        in_specs=(block, block, rows, rows, P(), P(), P(), P()),
        out_specs=(block, block, rows, rows, P(), P(), P()),
        check_vma=False,
    )
```

```python
import functools
import math

import jax
import jax.numpy as jnp
from jax import lax
from jax.experimental import pallas as pl
from jax.experimental.pallas import tpu as pltpu
from jax.sharding import PartitionSpec as P

HALF = 8
BF = jnp.bfloat16
F32 = jnp.float32


def busy(microseconds, megabytes):
    return pl.CostEstimate(
        flops=int(microseconds * 0.5e8), bytes_accessed=int(megabytes * 0.6e6), transcendentals=0
    )


def swapped(x, axis, flip):
    count = 1
    for name in (axis,) if isinstance(axis, str) else axis:
        count = count * lax.axis_size(name)
    return lax.ppermute(x, axis, [(i, i ^ flip) for i in range(count)])


def window_partner(x):
    count = lax.axis_size("seq")
    pairs = [(i, (i + 1) % count if i % 2 else (i - 1) % count) for i in range(count)]
    return lax.ppermute(x, "seq", pairs)


def edge_partner(x):
    count = lax.axis_size("seq")
    pairs = [(i, i + 1) for i in range(1, count - 1, 2)]
    return lax.ppermute(x, "seq", pairs + [(j, i) for i, j in pairs])


def with_halo(x, inner, outer, core):
    low = core == 0
    return jnp.concatenate(
        [jnp.where(low, outer, inner)[None], x, jnp.where(low, inner, outer)[None]], axis=0
    )


def tap_sum(padded, weight, slab_depth, height, grid_width, flipped):
    summed = jnp.zeros((slab_depth, height, grid_width, padded.shape[-1]), F32)
    for a in range(3):
        for b in range(3):
            for e in range(3):
                starts = (2 - a, 2 - b, 2 - e) if flipped else (a, b, e)
                part = padded[
                    starts[0] : starts[0] + slab_depth,
                    starts[1] : starts[1] + height,
                    starts[2] : starts[2] + grid_width,
                ]
                summed = summed + weight[9 * a + 3 * b + e] * part.astype(F32)
    return summed


OVER_ROWS = (((0,), (0,)), ((), ()))
OVER_LANES = (((1,), (1,)), ((), ()))


def allowed_pairs(nums, n):
    rows_shift, cols_shift, second = nums[0], nums[1], nums[2]

    def code(dim):
        t = lax.broadcasted_iota(jnp.int32, (n, n), dim)
        first_bit = jnp.where(((t >> 3) & 7) < rows_shift, 2, 0)
        return first_bit + jnp.where((t & 7) < cols_shift, second, 0)

    return jnp.where(code(0) == code(1), 1.0, 0.0).astype(F32)


def project(nums, x, mine, low, got, other, group, qkv):
    channels = x.shape[1]
    half = channels // 2
    quarter = half // 2
    low_rows, low_core = nums[3] == 0, nums[4] == 0
    x = x.astype(F32)
    x_mine = jnp.where(low_rows, x[:, :half], x[:, half:])
    x_peer = jnp.where(low_rows, x[:, half:], x[:, :half])
    x_got = jnp.where(low_core, x_peer[:, :quarter], x_peer[:, quarter:]).astype(BF)
    x_other = jnp.where(low_core, x_peer[:, quarter:], x_peer[:, :quarter]).astype(BF)
    x_mine = x_mine.astype(BF)
    for part in range(3):
        own = slice(part * channels + low, part * channels + low + group)
        far = slice(own.start + channels, own.stop + channels)
        total = jnp.dot(x_mine, mine[:, own], preferred_element_type=F32)
        total = total + jnp.dot(x_got, got[:, far], preferred_element_type=F32)
        total = total + jnp.dot(x_other, other[:, far], preferred_element_type=F32)
        qkv[part * group : (part + 1) * group, :] = total.T.astype(BF)


def attend(head_dim, allowed, scale, base, group, qkv, ba, ba_low, att, back, gs):
    def unit(raw):
        inverse = lax.rsqrt(jnp.sum(raw * raw, axis=0, keepdims=True) + 1.0)
        return inverse, (raw * inverse).astype(BF)

    def radius_back(raw, inverse, grad):
        inner = jnp.sum(raw * grad, axis=0, keepdims=True)
        return grad * inverse - raw * (inner * (inverse * inverse * inverse))

    def one_head(h):
        def rows(start):
            return pl.ds(pl.multiple_of(start + h * head_dim, head_dim), head_dim)

        s = scale[base + h]
        qf = qkv[rows(0), :].astype(F32)
        kf = qkv[rows(group), :].astype(F32)
        v = qkv[rows(2 * group), :]
        b = ba[rows(ba_low), :]
        iq, uq = unit(qf)
        ik, uk = unit(kf)
        cosine = lax.dot_general(uk, uq, OVER_ROWS, preferred_element_type=F32)
        expo = jnp.exp(cosine * s) * allowed
        prob = expo * (1.0 / jnp.sum(expo, axis=0, keepdims=True))
        weights = prob.astype(BF)
        att[rows(0), :] = jnp.dot(v, weights, preferred_element_type=F32).astype(BF)
        back_prob = lax.dot_general(v, b, OVER_ROWS, preferred_element_type=F32)
        mean = jnp.sum(prob * back_prob, axis=0, keepdims=True)
        back_score = prob * (back_prob - mean)
        gs[pl.ds(h, 1), :] = jnp.sum(back_score * cosine, axis=0, keepdims=True)
        scaled = (back_score * s).astype(BF)
        buq = jnp.dot(uk, scaled, preferred_element_type=F32)
        buk = lax.dot_general(uq, scaled, OVER_LANES, preferred_element_type=F32)
        bv = lax.dot_general(b, weights, OVER_LANES, preferred_element_type=F32)
        back[rows(0), :] = radius_back(qf, iq, buq).astype(BF)
        back[rows(group), :] = radius_back(kf, ik, buk).astype(BF)
        back[rows(2 * group), :] = bv.astype(BF)

    def body(i, carry):
        for u in range(4):
            one_head(i * 4 + u)
        return carry

    lax.fori_loop(0, group // head_dim // 4, body, 0)


def first_kernel(group, head_dim, nums, scale, xm, xg, cot, order, w_qkv, w_proj, got, other, *outs):
    send, x_rows, att, ba, gs, qkv = outs
    channels = xm.shape[1]
    half = channels // 2
    x = jnp.concatenate([xm[...], xg[...]], axis=0)
    project(nums, x, w_qkv, 0, got, other, group, qkv)
    quarter = half // 2
    dp, core = nums[3], nums[4]

    def back_rows(start, count, weight):
        value = lax.dot_general(weight, cot[...], OVER_LANES, preferred_element_type=F32)
        ba[pl.ds(pl.multiple_of(start, quarter), count), :] = value.astype(BF)

    back_rows(dp * half, half, w_proj[...])
    back_rows((1 - dp) * half + core * quarter, quarter, got[:, :channels])
    back_rows((1 - dp) * half + (1 - core) * quarter, quarter, other[:, :channels])
    allowed = allowed_pairs(nums, x.shape[0])
    attend(head_dim, allowed, scale, 0, group, qkv, ba, 0, att, send, gs)
    x_rows[...] = lax.dot_general(
        order[:half, :], x, OVER_LANES, preferred_element_type=F32
    ).astype(BF)
    send[3 * group :, :] = lax.dot_general(
        order[half:, :], x, OVER_LANES, preferred_element_type=F32
    ).astype(BF)


def second_kernel(group, head_dim, nums, scale, xm, xg, order, w_qkv, got, other, ba, att_first, *outs):
    send, att_rows, att, gs, qkv = outs
    channels = xm.shape[1]
    half = channels // 2
    low = channels - group
    x = jnp.concatenate([xm[...], xg[...]], axis=0)
    project(nums, x, w_qkv, low, got, other, group, qkv)
    allowed = allowed_pairs(nums, x.shape[0])
    attend(head_dim, allowed, scale, low // head_dim, group, qkv, ba, low, att, send, gs)

    def ordered(rows):
        total = jnp.dot(order[rows, :low], att_first[...], preferred_element_type=F32)
        total = total + jnp.dot(order[rows, low:], att[...], preferred_element_type=F32)
        return total.astype(BF)

    att_rows[...] = ordered(slice(0, half))
    send[3 * group :, :] = ordered(slice(half, channels))


def attention_call(body, name, group, head_dim, head_count, outs, operands):
    n = 2 * operands[2].shape[0]
    channels = operands[2].shape[1]
    vmem = pl.BlockSpec(memory_space=pltpu.VMEM)
    smem = pl.BlockSpec(memory_space=pltpu.SMEM)
    shapes = tuple(jax.ShapeDtypeStruct((rows, n), BF) for rows in outs)
    shapes = shapes + (jax.ShapeDtypeStruct((group // head_dim, n), F32),)
    return pl.pallas_call(
        functools.partial(body, group, head_dim),
        out_shape=shapes,
        in_specs=[smem, smem] + [vmem] * (len(operands) - 2),
        out_specs=(vmem,) * len(shapes),
        scratch_shapes=[pltpu.VMEM((3 * group, n), BF)],
        compiler_params=pltpu.CompilerParams(vmem_limit_bytes=20 * 1024 * 1024),
        cost_estimate=busy(5 + 0.5 * (group // head_dim), 8),
        name=name,
    )(*operands)


def stage_kernel(core, w_qkv, w_proj, tokens, weights, inner, outer, sems):
    rows, channels = weights.shape[0], w_proj.shape[1]
    mine = pl.ds(pl.multiple_of(core[0] * rows, rows), rows)
    copies = (
        (w_proj.at[mine, :], weights.at[:, :channels]),
        (w_qkv.at[mine, :], weights.at[:, channels:]),
        (tokens.at[0, core[0]], outer),
        (tokens.at[0, 1 - core[0]], inner),
    )
    started = [pltpu.make_async_copy(x, y, sems.at[i]) for i, (x, y) in enumerate(copies)]
    for copy in started:
        copy.start()
    for copy in started:
        copy.wait()


def stage(core, w_qkv, w_proj, tokens):
    channels = w_proj.shape[1]
    rows = w_proj.shape[0] // 2
    anywhere = pl.BlockSpec(memory_space=pl.ANY)
    vmem = pl.BlockSpec(memory_space=pltpu.VMEM)
    plane = jax.ShapeDtypeStruct(tokens.shape[2:], BF)
    return pl.pallas_call(
        stage_kernel,
        out_shape=(jax.ShapeDtypeStruct((rows, 4 * channels), BF), plane, plane),
        in_specs=[pl.BlockSpec(memory_space=pltpu.SMEM)] + [anywhere] * 3,
        out_specs=(vmem,) * 3,
        scratch_shapes=[pltpu.SemaphoreType.DMA((4,))],
        cost_estimate=busy(2.5, 4),
        name="stage",
    )(core[None].astype(jnp.int32), w_qkv, w_proj, tokens)


def back_kernel(group, nums, first, second, w_qkv, got, other, att1, att2, *outs):
    mine, send, att_mine = outs
    n = first.shape[1]
    half = n // 2
    channels = att_mine.shape[1]
    rest = channels - group
    low_rows, low_core = nums[3] == 0, nums[4] == 0
    first_t = first[: 3 * group, :].astype(F32).T.astype(BF)
    second_t = second[: 3 * rest, :].astype(F32).T.astype(BF)

    def through(pieces):
        total = None
        for left, right in pieces:
            term = lax.dot_general(left, right, OVER_LANES, preferred_element_type=F32)
            total = term if total is None else total + term
        return total

    def pieces(weight, base):
        for part in range(3):
            low = base + part * channels
            yield first_t[:, part * group : (part + 1) * group], weight[:, low : low + group]
            yield second_t[:, part * rest : (part + 1) * rest], weight[:, low + group : low + channels]

    from_mine = through(pieces(w_qkv, 0))
    from_got = through(pieces(got, channels))
    from_other = through(pieces(other, channels))
    from_peer = jnp.concatenate(
        [jnp.where(low_core, from_got, from_other), jnp.where(low_core, from_other, from_got)], axis=1
    )
    shifted = jnp.concatenate(
        [jnp.where(low_rows, from_mine, from_peer), jnp.where(low_rows, from_peer, from_mine)], axis=1
    ).astype(BF)
    mine[...] = shifted[:half]
    send[:half, :] = shifted[half:]
    for low, ref in ((0, att1), (group, att2)):
        wide = slice(low, low + ref.shape[0])
        turned = ref[...].astype(F32).T.astype(BF)
        att_mine[:, wide] = turned[:half]
        send[half:, wide] = turned[half:]


def back_through(group, operands):
    n = operands[1].shape[1]
    channels = operands[6].shape[0] + operands[7].shape[0]
    vmem = pl.BlockSpec(memory_space=pltpu.VMEM)
    smem = pl.BlockSpec(memory_space=pltpu.SMEM)
    half = jax.ShapeDtypeStruct((n // 2, channels), BF)
    return pl.pallas_call(
        functools.partial(back_kernel, group),
        out_shape=(half, jax.ShapeDtypeStruct((n, channels), BF), half),
        in_specs=[smem] + [vmem] * (len(operands) - 1),
        out_specs=(vmem,) * 3,
        compiler_params=pltpu.CompilerParams(vmem_limit_bytes=20 * 1024 * 1024),
        cost_estimate=busy(4, 8),
        name="back_through",
    )(*operands)


def after(x, *others):
    anywhere = pl.BlockSpec(memory_space=pl.ANY)

    def nothing(*refs):
        del refs

    return pl.pallas_call(
        nothing,
        out_shape=jax.ShapeDtypeStruct(x.shape, x.dtype),
        in_specs=[anywhere] * (1 + len(others)),
        out_specs=anywhere,
        input_output_aliases={0: 0},
        name="ordered",
    )(x, *others)


def pick(x, index, axis):
    return lax.dynamic_index_in_dim(x, index, axis, keepdims=False)


def tree_sum(parts):
    while len(parts) > 1:
        parts = [a + b for a, b in zip(parts[::2], parts[1::2])]
    return parts[0]


def chip_stages(chips):
    stages = []
    stride = 1
    while stride < chips:
        radix = 4 if (chips // stride) % 4 == 0 else 2
        stages.append((radix, stride))
        stride = stride * radix
    return stages


class Place:
    def __init__(self, channels):
        self.seq = lax.axis_index("seq")
        self.core = self.seq % 2
        self.rep, self.dp = lax.axis_index("rep"), lax.axis_index("dp")
        self.stages = chip_stages(lax.axis_size("seq") // 2)
        self.split = self.stages[0][0] if self.stages else 1
        self.digit = (self.seq // 2) % self.split
        self.rows = channels // (8 * self.split)
        self.channels = channels

    def row_order(self):
        p = jnp.arange(self.channels)
        inner = p % self.rows
        z = (p // self.rows) % self.split
        square = (p // (self.rows * self.split)) % 4
        pair = p // (self.rows * self.split * 4)
        rep, dp = self.rep ^ (square >> 1), self.dp ^ (square & 1)
        target = ((dp * 2 + (self.core ^ pair)) * 2 + rep) * self.split + (self.digit ^ z)
        target = target * self.rows + inner
        return (target[:, None] == jnp.arange(self.channels)[None, :]).astype(BF)


def gradient_kernel(width, has_proj, *refs):
    if has_proj:
        xm, xg, bm, bg, am, cm, cg, own, s1, s2, s3 = refs
    else:
        xm, xg, bm, bg, own, s1, s2, s3 = refs
    quarter = own.shape[0]
    tile = 384
    x_far = xg[xg.shape[0] - 4 * quarter :, :]

    def put(first, total):
        columns = slice(first, first + tile)
        own[:, columns] = total[:quarter]
        for k, ref in enumerate((s1, s2, s3)):
            ref[:, columns] = total[(k + 1) * quarter : (k + 2) * quarter].astype(BF)

    for first in range(0, width, tile):
        rows = slice(first, first + tile)
        total = lax.dot_general(xm[...], bm[rows, :], OVER_LANES, preferred_element_type=F32)
        put(first, total + lax.dot_general(x_far, bg[rows, :], OVER_LANES, preferred_element_type=F32))
    if has_proj:
        far = bg[width:, :]
        for first in range(0, cm.shape[1], tile):
            columns = slice(first, first + tile)
            total = jnp.dot(am[...], cm[:, columns], preferred_element_type=F32)
            put(width + first, total + jnp.dot(far, cg[:, columns], preferred_element_type=F32))


def chip_gradient(operands):
    rows, n = operands[0].shape
    width = operands[2].shape[0] - rows
    has_proj = len(operands) > 4
    total = width + (operands[5].shape[1] if has_proj else 0)
    vmem = pl.BlockSpec(memory_space=pltpu.VMEM)
    wire = jax.ShapeDtypeStruct((rows // 4, total), BF)
    return pl.pallas_call(
        functools.partial(gradient_kernel, width, has_proj),
        out_shape=(jax.ShapeDtypeStruct((rows // 4, total), F32), wire, wire, wire),
        in_specs=[vmem] * len(operands),
        out_specs=(vmem,) * 4,
        compiler_params=pltpu.CompilerParams(vmem_limit_bytes=16 * 1024 * 1024),
        cost_estimate=busy(1.5, 3.5),
        name="chip_gradient",
    )(*operands)


def sum_square(own, sends, place):
    got = [own] + [swapped(s, ("rep", "dp"), k + 1).astype(F32) for k, s in enumerate(sends)]
    return tree_sum(got)


def sum_chips(total, place, *others):
    parts = total.reshape(place.split, place.rows, -1)
    got = [parts[0]]
    for k in range(1, place.split):
        there = swapped(parts[k].astype(BF), "seq", 2 * k)
        got.append((after(there, *others) if others else there).astype(F32))
    total = tree_sum(got)
    for radix, stride in place.stages[1:]:
        held = total.astype(BF)
        got = [swapped(held, "seq", 2 * k * stride) if k else held for k in range(radix)]
        total = tree_sum([g.astype(F32) for g in got])
    return total.astype(BF)


def gather_blocks(block, place):
    got = [swapped(block, "seq", 2 * k) if k else block for k in range(place.split)]
    chips = jnp.concatenate(got)
    other_rep = swapped(chips, "rep", 1)
    return chips, other_rep, swapped(chips, "seq", 1), swapped(other_rep, "seq", 1)


def assemble_kernel(split, factor, group, at, *refs):
    first, second = refs[:4], refs[4:8]
    qkv, proj = refs[8], refs[9]
    rows = first[0].shape[0] // split
    third = qkv.shape[1] // 3
    rest = third - group
    for pair in range(2):
        for square in range(2):
            index = 2 * pair + square
            base = ((at[0] ^ pair) * 2 + (at[1] ^ square)) * split
            for z in range(split):
                here = slice(z * rows, (z + 1) * rows)
                there = pl.ds(pl.multiple_of((base + (at[2] ^ z)) * rows, rows), rows)
                for part in range(3):
                    low, mid = part * third, part * third + group
                    a = first[index][here, part * group : (part + 1) * group]
                    qkv[there, low:mid] = a.astype(F32) * factor
                    b = second[index][here, part * rest : (part + 1) * rest]
                    qkv[there, mid : low + third] = b.astype(F32) * factor
                proj[there, :] = second[index][here, 3 * rest :].astype(F32) * factor


def assemble(first, second, place, factor, group):
    rows = 4 * first[0].shape[0]
    channels = place.channels
    vmem = pl.BlockSpec(memory_space=pltpu.VMEM)
    smem = pl.BlockSpec(memory_space=pltpu.SMEM)
    at = jnp.stack([place.core, place.rep, place.digit]).astype(jnp.int32)
    return pl.pallas_call(
        functools.partial(assemble_kernel, place.split, factor, group),
        out_shape=(
            jax.ShapeDtypeStruct((rows, 3 * channels), F32),
            jax.ShapeDtypeStruct((rows, channels), F32),
        ),
        in_specs=[smem] + [vmem] * 8,
        out_specs=(vmem, vmem),
        compiler_params=pltpu.CompilerParams(vmem_limit_bytes=16 * 1024 * 1024),
        cost_estimate=busy(3, 7),
        name="assemble",
    )(at, *first, *second)


def sum_everywhere(x, place):
    half = x.shape[0] // 2
    low = place.core == 0
    x = jnp.where(low, x[:half], x[half:]) + swapped(
        jnp.where(low, x[half:], x[:half]), "seq", 1
    )
    x = x + swapped(x, "rep", 1)
    x = x + swapped(x, "dp", 1)
    flip = 2
    while flip < lax.axis_size("seq"):
        x = x + swapped(x, "seq", flip)
        flip = flip * 2
    got = swapped(x, "seq", 1)
    return jnp.concatenate([jnp.where(low, x, got), jnp.where(low, got, x)])


def rows_of_both(mine, got, other, place):
    half = got.shape[0]
    m0, m1 = mine[:half], mine[half:]
    p0 = jnp.where(place.core == 0, got, other)
    p1 = jnp.where(place.core == 0, other, got)
    low = place.dp == 0
    return jnp.concatenate(
        [jnp.where(low, a, b) for a, b in ((m0, p0), (m1, p1), (p0, m0), (p1, m1))]
    )


GROUP_HEADS = 16


def tap_gradient_kernel(bm, tokens, back, unit, scale, out):
    depth, height, width, lanes = bm.shape
    mixed = bm[...]
    zero = jnp.zeros((1, lanes), F32)
    for e in range(3):
        shifted = tokens[:, :, e : e + width, :].astype(F32)
        for a in range(3):
            for b in range(3):
                product = mixed * shifted[a : a + depth, b : b + height]
                row = jnp.sum(jnp.sum(product, axis=(0, 1)), axis=0, keepdims=True)
                out[9 * a + 3 * b + e : 9 * a + 3 * b + e + 1, :] = row
    gain = jnp.sum(jnp.sum(back[...].astype(F32) * unit[...], axis=(0, 1)), axis=0, keepdims=True)
    out[27:28, :] = gain
    sums = jnp.sum(scale[...], axis=1, keepdims=True)
    heads = sums.shape[0]
    same = lax.broadcasted_iota(jnp.int32, (heads, lanes), 0) == lax.broadcasted_iota(
        jnp.int32, (heads, lanes), 1
    )
    out[28:29, :] = jnp.sum(jnp.where(same, sums, 0.0), axis=0, keepdims=True)
    for row in range(29, 32):
        out[row : row + 1, :] = zero


def small_gradients(bm, padded, back, unit, scale):
    depth, height, width, channels = bm.shape
    tile = 128

    def field(x):
        return pl.BlockSpec(x.shape[:-1] + (tile,), lambda i: (0, 0, 0, i))

    return pl.pallas_call(
        tap_gradient_kernel,
        grid=(channels // tile,),
        out_shape=jax.ShapeDtypeStruct((32, channels), F32),
        in_specs=[
            field(bm),
            field(padded),
            field(back),
            field(unit),
            pl.BlockSpec(scale.shape, lambda i: (0, 0)),
        ],
        out_specs=pl.BlockSpec((32, tile), lambda i: (0, i)),
        compiler_params=pltpu.CompilerParams(vmem_limit_bytes=16 * 1024 * 1024),
        cost_estimate=busy(3.5, 3),
        name="small_gradients",
    )(bm, padded, back, unit, scale)


def per_device(tokens, cotangent, w_qkv, w_proj, conv_weight, norm_gain, head_scale, shift_offsets):
    slab = tokens[0]
    cot = cotangent[0]
    depth, height, width, channels = slab.shape
    head_count = head_scale.shape[0]
    head_dim = channels // head_count
    place = Place(channels)
    core, dp = place.core, place.dp
    rows_shift, cols_shift = shift_offsets[0], shift_offsets[1]
    positions = depth * height * width
    half = positions // 2
    columns = jnp.arange(HALF)[None, None, :, None]
    straight = (columns >= cols_shift) == (core == 1)
    group = GROUP_HEADS * head_dim

    def split_columns(field):
        low, high = field[:, :, :HALF], field[:, :, HALF:]
        return (
            jnp.where(straight, low, high).reshape(half, -1),
            jnp.where(straight, high, low).reshape(half, -1),
        )

    def join_columns(mine, theirs):
        mine = mine.reshape(depth, height, HALF, -1)
        theirs = theirs.reshape(depth, height, HALF, -1)
        return jnp.concatenate(
            [jnp.where(straight, mine, theirs), jnp.where(straight, theirs, mine)], axis=2
        )

    spatial = ((0, 0), (1, 1), (1, 1), (0, 0))
    weights_part, inner, outer = stage(core, w_qkv, w_proj, tokens)
    outer = edge_partner(outer)
    inner = swapped(inner, "seq", 1)
    weights_got = swapped(weights_part, "dp", 1)
    cot_mine, cot_theirs = split_columns(cot)
    cot_got = window_partner(cot_theirs)
    padded_tokens = jnp.pad(with_halo(slab, inner, after(outer, cot_got), core), spatial)
    cot_window = jnp.concatenate([cot_mine, cot_got])
    order = place.row_order()

    mixed_field = slab.astype(F32) + tap_sum(
        padded_tokens, conv_weight, depth, height, width, False
    )
    centred = mixed_field - jnp.mean(mixed_field, axis=-1, keepdims=True)
    inverse_std = lax.rsqrt(jnp.mean(centred * centred, axis=-1, keepdims=True) + 1e-05)
    unit_field = centred * inverse_std
    normed = (unit_field * norm_gain).astype(BF)
    x_mine, x_theirs = split_columns(normed)
    x_theirs = window_partner(x_theirs)
    weights_got = after(weights_got, x_theirs)
    weights_other = swapped(weights_got, "seq", 1)
    cot_other = swapped(cot_window, "seq", 1)
    nums = jnp.stack([rows_shift, cols_shift, 1 - core, dp, core]).astype(jnp.int32)
    half_rows = channels // 2
    send_first, x_rows, att_first, back_attended, scale_first = attention_call(
        first_kernel,
        "first_heads",
        group,
        head_dim,
        head_count,
        (3 * group + half_rows, half_rows, group, channels),
        (nums, head_scale, x_mine, x_theirs, cot_window, order, w_qkv, w_proj, weights_got, weights_other),
    )
    got_first = swapped(send_first, "seq", 1)
    own, *sends = chip_gradient((x_rows, got_first, send_first, got_first))
    rest = channels - group
    send_second, att_rows, att_second, scale_second = attention_call(
        second_kernel,
        "second_heads",
        rest,
        head_dim,
        head_count,
        (3 * rest + half_rows, half_rows, rest),
        (
            nums,
            head_scale,
            x_mine,
            x_theirs,
            order,
            w_qkv,
            weights_got,
            weights_other,
            after(back_attended, own),
            att_first,
        ),
    )
    first_total = sum_square(own, sends, place)

    got_second = swapped(send_second, "seq", 1)
    own, *sends = chip_gradient(
        (x_rows, got_first, send_second, got_second, att_rows, cot_window, cot_other)
    )
    second_total = sum_square(own, sends, place)
    first_block = sum_chips(first_total, place, own)
    second_block = sum_chips(second_total, place)
    factor = 1.0 / math.sqrt(
        lax.axis_size("rep") * lax.axis_size("dp") * lax.axis_size("seq") * positions
    )
    grad_qkv, grad_proj = assemble(
        gather_blocks(first_block, place), gather_blocks(second_block, place), place, factor, group
    )

    back_mine, window_send, att_mine = back_through(
        group,
        (
            nums,
            send_first,
            send_second,
            w_qkv,
            weights_got,
            weights_other,
            att_first,
            att_second,
        ),
    )
    window_send = after(window_partner(window_send), own, first_total)
    back_normed = join_columns(back_mine, window_send[:half])
    restored = join_columns(att_mine, window_send[half:]).reshape(positions, channels)
    full_proj = rows_of_both(
        w_proj, weights_got[:, :channels], weights_other[:, :channels], place
    )
    projected = jnp.dot(restored, full_proj, preferred_element_type=F32)
    output = (mixed_field + projected.reshape(slab.shape)).astype(BF)

    back_float = back_normed.astype(F32)
    grad_unit = back_float * norm_gain
    back_mixed = cot.astype(F32) + inverse_std * (
        grad_unit
        - jnp.mean(grad_unit, axis=-1, keepdims=True)
        - unit_field * jnp.mean(grad_unit * unit_field, axis=-1, keepdims=True)
    )
    edges = back_mixed.astype(BF)
    inner = swapped(pick(edges, 1 - core, 0), "seq", 1)
    outer = edge_partner(pick(edges, core, 0))
    padded_back = jnp.pad(
        with_halo(back_mixed, inner.astype(F32), outer.astype(F32), core), spatial
    )
    grad_tokens = (
        back_mixed + tap_sum(padded_back, conv_weight, depth, height, width, True)
    ).astype(BF)
    scale_rows = jnp.concatenate([scale_first, scale_second])
    small = small_gradients(back_mixed, padded_tokens, back_normed, unit_field, scale_rows)
    small = sum_everywhere(after(small, second_total), place) * factor
    taps = conv_weight.shape[0]
    return (
        output[None],
        grad_tokens[None],
        grad_qkv,
        grad_proj,
        small[:taps],
        small[taps],
        small[taps + 1, :head_count],
    )


def solution(mesh):
    block = P(("rep", "dp"), "seq", None, None, None)
    rows = P("dp", None)
    return jax.shard_map(
        per_device,
        mesh=mesh,
        in_specs=(block, block, rows, rows, P(), P(), P(), P()),
        out_specs=(block, block, rows, rows, P(), P(), P()),
        check_vma=False,
    )
```

```python
import functools
import math

import jax
import jax.numpy as jnp
from jax import lax
from jax.experimental import pallas as pl
from jax.experimental.pallas import tpu as pltpu
from jax.sharding import PartitionSpec as P

HALF = 8
LOG2_E = math.log2(math.e)
BF = jnp.bfloat16
F32 = jnp.float32


def busy(microseconds, megabytes):
    return pl.CostEstimate(
        flops=int(microseconds * 0.5e7), bytes_accessed=int(megabytes * 0.1e6), transcendentals=0
    )


def swapped(x, axis, flip):
    count = 1
    for name in (axis,) if isinstance(axis, str) else axis:
        count = count * lax.axis_size(name)
    return lax.ppermute(x, axis, [(i, i ^ flip) for i in range(count)])


def window_partner(x):
    count = lax.axis_size("seq")
    pairs = [(i, (i + 1) % count if i % 2 else (i - 1) % count) for i in range(count)]
    return lax.ppermute(x, "seq", pairs)


def edge_partner(x):
    count = lax.axis_size("seq")
    pairs = [(i, i + 1) for i in range(1, count - 1, 2)]
    return lax.ppermute(x, "seq", pairs + [(j, i) for i, j in pairs])


def with_halo(x, inner, outer, core):
    low = core == 0
    return jnp.concatenate(
        [jnp.where(low, outer, inner)[None], x, jnp.where(low, inner, outer)[None]], axis=0
    )


def tap_sum(padded, weight, slab_depth, height, grid_width, flipped):
    summed = jnp.zeros((slab_depth, height, grid_width, padded.shape[-1]), F32)
    for a in range(3):
        for b in range(3):
            for e in range(3):
                starts = (2 - a, 2 - b, 2 - e) if flipped else (a, b, e)
                part = padded[
                    starts[0] : starts[0] + slab_depth,
                    starts[1] : starts[1] + height,
                    starts[2] : starts[2] + grid_width,
                ]
                summed = summed + weight[9 * a + 3 * b + e] * part.astype(F32)
    return summed


OVER_ROWS = (((0,), (0,)), ((), ()))
OVER_LANES = (((1,), (1,)), ((), ()))


def allowed_pairs(nums, n):
    rows_shift, cols_shift, second = nums[0], nums[1], nums[2]

    def code(dim):
        t = lax.broadcasted_iota(jnp.int32, (n, n), dim)
        first_bit = jnp.where(((t >> 3) & 7) < rows_shift, 2, 0)
        return first_bit + jnp.where((t & 7) < cols_shift, second, 0)

    return jnp.where(code(0) == code(1), 1.0, 0.0).astype(F32)


def project(nums, x, mine, low, got, other, group, qkv):
    channels = x.shape[1]
    half = channels // 2
    quarter = half // 2
    low_rows, low_core = nums[3] == 0, nums[4] == 0
    x = x.astype(F32)
    x_mine = jnp.where(low_rows, x[:, :half], x[:, half:])
    x_peer = jnp.where(low_rows, x[:, half:], x[:, :half])
    x_got = jnp.where(low_core, x_peer[:, :quarter], x_peer[:, quarter:]).astype(BF)
    x_other = jnp.where(low_core, x_peer[:, quarter:], x_peer[:, :quarter]).astype(BF)
    x_mine = x_mine.astype(BF)
    for part in range(3):
        own = slice(part * channels + low, part * channels + low + group)
        far = slice(own.start + channels, own.stop + channels)
        total = jnp.dot(x_mine, mine[:, own], preferred_element_type=F32)
        total = total + jnp.dot(x_got, got[:, far], preferred_element_type=F32)
        total = total + jnp.dot(x_other, other[:, far], preferred_element_type=F32)
        qkv[part * group : (part + 1) * group, :] = total.T.astype(BF)


def attend(head_dim, allowed, scale, base, group, qkv, ba, ba_low, att, back, gs):
    def unit(raw):
        inverse = lax.rsqrt(jnp.sum(raw * raw, axis=0, keepdims=True) + 1.0)
        return inverse, (raw * inverse).astype(BF)

    def radius_back(raw, inverse, grad):
        inner = jnp.sum(raw * grad, axis=0, keepdims=True)
        return grad * inverse - raw * (inner * (inverse * inverse * inverse))

    def one_head(h):
        def rows(start):
            return pl.ds(pl.multiple_of(start + h * head_dim, head_dim), head_dim)

        s = scale[base + h]
        qf = qkv[rows(0), :].astype(F32)
        kf = qkv[rows(group), :].astype(F32)
        v = qkv[rows(2 * group), :]
        b = ba[rows(ba_low), :]
        iq, uq = unit(qf)
        ik, uk = unit(kf)
        cosine = lax.dot_general(uk, uq, OVER_ROWS, preferred_element_type=F32)
        back_prob = lax.dot_general(v, b, OVER_ROWS, preferred_element_type=F32)
        expo = jnp.exp2(cosine * (s * LOG2_E)) * allowed
        inverse = 1.0 / jnp.sum(expo, axis=0, keepdims=True)
        weights = (expo * inverse).astype(BF)
        att[rows(0), :] = jnp.dot(v, weights, preferred_element_type=F32).astype(BF)
        mean = jnp.sum(expo * back_prob, axis=0, keepdims=True) * inverse
        scaled = expo * (inverse * s) * (back_prob - mean)
        gs[pl.ds(h, 1), :] = jnp.sum(scaled * cosine, axis=0, keepdims=True) * (1.0 / s)
        scaled = scaled.astype(BF)
        buq = jnp.dot(uk, scaled, preferred_element_type=F32)
        buk = lax.dot_general(uq, scaled, OVER_LANES, preferred_element_type=F32)
        bv = lax.dot_general(b, weights, OVER_LANES, preferred_element_type=F32)
        back[rows(0), :] = radius_back(qf, iq, buq).astype(BF)
        back[rows(group), :] = radius_back(kf, ik, buk).astype(BF)
        back[rows(2 * group), :] = bv.astype(BF)

    def body(i, carry):
        for u in range(8):
            one_head(i * 8 + u)
        return carry

    lax.fori_loop(0, group // head_dim // 8, body, 0)


def first_kernel(group, head_dim, nums, scale, xm, xg, cot, order, w_qkv, w_proj, got, other, *outs):
    send, x_rows, att, ba, gs, qkv = outs
    channels = xm.shape[1]
    half = channels // 2
    x = jnp.concatenate([xm[...], xg[...]], axis=0)
    project(nums, x, w_qkv, 0, got, other, group, qkv)
    quarter = half // 2
    dp, core = nums[3], nums[4]

    def back_rows(start, count, weight):
        value = lax.dot_general(weight, cot[...], OVER_LANES, preferred_element_type=F32)
        ba[pl.ds(pl.multiple_of(start, quarter), count), :] = value.astype(BF)

    back_rows(dp * half, half, w_proj[...])
    back_rows((1 - dp) * half + core * quarter, quarter, got[:, :channels])
    back_rows((1 - dp) * half + (1 - core) * quarter, quarter, other[:, :channels])
    allowed = allowed_pairs(nums, x.shape[0])
    attend(head_dim, allowed, scale, 0, group, qkv, ba, 0, att, send, gs)
    x_rows[...] = lax.dot_general(
        order[:half, :], x, OVER_LANES, preferred_element_type=F32
    ).astype(BF)
    send[3 * group :, :] = lax.dot_general(
        order[half:, :], x, OVER_LANES, preferred_element_type=F32
    ).astype(BF)


def second_kernel(group, head_dim, nums, scale, xm, xg, order, w_qkv, got, other, ba, att_first, *outs):
    send, att_rows, att, gs, qkv = outs
    channels = xm.shape[1]
    half = channels // 2
    low = channels - group
    x = jnp.concatenate([xm[...], xg[...]], axis=0)
    project(nums, x, w_qkv, low, got, other, group, qkv)
    allowed = allowed_pairs(nums, x.shape[0])
    attend(head_dim, allowed, scale, low // head_dim, group, qkv, ba, low, att, send, gs)

    def ordered(rows):
        total = jnp.dot(order[rows, :low], att_first[...], preferred_element_type=F32)
        total = total + jnp.dot(order[rows, low:], att[...], preferred_element_type=F32)
        return total.astype(BF)

    att_rows[...] = ordered(slice(0, half))
    send[3 * group :, :] = ordered(slice(half, channels))


def attention_call(body, name, group, head_dim, head_count, outs, operands):
    n = 2 * operands[2].shape[0]
    channels = operands[2].shape[1]
    vmem = pl.BlockSpec(memory_space=pltpu.VMEM)
    smem = pl.BlockSpec(memory_space=pltpu.SMEM)
    shapes = tuple(jax.ShapeDtypeStruct((rows, n), BF) for rows in outs)
    shapes = shapes + (jax.ShapeDtypeStruct((group // head_dim, n), F32),)
    return pl.pallas_call(
        functools.partial(body, group, head_dim),
        out_shape=shapes,
        in_specs=[smem, smem] + [vmem] * (len(operands) - 2),
        out_specs=(vmem,) * len(shapes),
        scratch_shapes=[pltpu.VMEM((3 * group, n), BF)],
        compiler_params=pltpu.CompilerParams(vmem_limit_bytes=60 * 1024 * 1024),
        cost_estimate=busy(5 + 0.5 * (group // head_dim), 8),
        name=name,
    )(*operands)


def stage_kernel(core, w_qkv, w_proj, tokens, weights, inner, outer, sems):
    rows, channels = weights.shape[0], w_proj.shape[1]
    mine = pl.ds(pl.multiple_of(core[0] * rows, rows), rows)
    copies = (
        (w_proj.at[mine, :], weights.at[:, :channels]),
        (w_qkv.at[mine, :], weights.at[:, channels:]),
        (tokens.at[0, core[0]], outer),
        (tokens.at[0, 1 - core[0]], inner),
    )
    started = [pltpu.make_async_copy(x, y, sems.at[i]) for i, (x, y) in enumerate(copies)]
    for copy in started:
        copy.start()
    for copy in started:
        copy.wait()


def stage(core, w_qkv, w_proj, tokens):
    channels = w_proj.shape[1]
    rows = w_proj.shape[0] // 2
    anywhere = pl.BlockSpec(memory_space=pl.ANY)
    vmem = pl.BlockSpec(memory_space=pltpu.VMEM)
    plane = jax.ShapeDtypeStruct(tokens.shape[2:], BF)
    return pl.pallas_call(
        stage_kernel,
        out_shape=(jax.ShapeDtypeStruct((rows, 4 * channels), BF), plane, plane),
        in_specs=[pl.BlockSpec(memory_space=pltpu.SMEM)] + [anywhere] * 3,
        out_specs=(vmem,) * 3,
        scratch_shapes=[pltpu.SemaphoreType.DMA((4,))],
        cost_estimate=busy(2.5, 4),
        name="stage",
    )(core[None].astype(jnp.int32), w_qkv, w_proj, tokens)


def back_kernel(group, nums, first, second, w_qkv, got, other, att1, att2, *outs):
    mine, send, att_mine = outs
    n = first.shape[1]
    half = n // 2
    channels = att_mine.shape[1]
    rest = channels - group
    low_rows, low_core = nums[3] == 0, nums[4] == 0
    first_t = first[: 3 * group, :].astype(F32).T.astype(BF)
    second_t = second[: 3 * rest, :].astype(F32).T.astype(BF)

    def through(pieces):
        total = None
        for left, right in pieces:
            term = lax.dot_general(left, right, OVER_LANES, preferred_element_type=F32)
            total = term if total is None else total + term
        return total

    def pieces(weight, base):
        for part in range(3):
            low = base + part * channels
            yield first_t[:, part * group : (part + 1) * group], weight[:, low : low + group]
            yield second_t[:, part * rest : (part + 1) * rest], weight[:, low + group : low + channels]

    from_mine = through(pieces(w_qkv, 0))
    from_got = through(pieces(got, channels))
    from_other = through(pieces(other, channels))
    from_peer = jnp.concatenate(
        [jnp.where(low_core, from_got, from_other), jnp.where(low_core, from_other, from_got)], axis=1
    )
    shifted = jnp.concatenate(
        [jnp.where(low_rows, from_mine, from_peer), jnp.where(low_rows, from_peer, from_mine)], axis=1
    ).astype(BF)
    mine[...] = shifted[:half]
    send[:half, :] = shifted[half:]
    for low, ref in ((0, att1), (group, att2)):
        wide = slice(low, low + ref.shape[0])
        turned = ref[...].astype(F32).T.astype(BF)
        att_mine[:, wide] = turned[:half]
        send[half:, wide] = turned[half:]


def back_through(group, operands):
    n = operands[1].shape[1]
    channels = operands[6].shape[0] + operands[7].shape[0]
    vmem = pl.BlockSpec(memory_space=pltpu.VMEM)
    smem = pl.BlockSpec(memory_space=pltpu.SMEM)
    half = jax.ShapeDtypeStruct((n // 2, channels), BF)
    return pl.pallas_call(
        functools.partial(back_kernel, group),
        out_shape=(half, jax.ShapeDtypeStruct((n, channels), BF), half),
        in_specs=[smem] + [vmem] * (len(operands) - 1),
        out_specs=(vmem,) * 3,
        compiler_params=pltpu.CompilerParams(vmem_limit_bytes=60 * 1024 * 1024),
        cost_estimate=busy(4, 8),
        name="back_through",
    )(*operands)


def after(x, *others):
    anywhere = pl.BlockSpec(memory_space=pl.ANY)

    def nothing(*refs):
        del refs

    return pl.pallas_call(
        nothing,
        out_shape=jax.ShapeDtypeStruct(x.shape, x.dtype),
        in_specs=[anywhere] * (1 + len(others)),
        out_specs=anywhere,
        input_output_aliases={0: 0},
        name="ordered",
    )(x, *others)


def pick(x, index, axis):
    return lax.dynamic_index_in_dim(x, index, axis, keepdims=False)


def tree_sum(parts):
    while len(parts) > 1:
        parts = [a + b for a, b in zip(parts[::2], parts[1::2])]
    return parts[0]


def chip_stages(chips):
    stages = []
    stride = 1
    while stride < chips:
        radix = 4 if (chips // stride) % 4 == 0 else 2
        stages.append((radix, stride))
        stride = stride * radix
    return stages


class Place:
    def __init__(self, channels):
        self.seq = lax.axis_index("seq")
        self.core = self.seq % 2
        self.rep, self.dp = lax.axis_index("rep"), lax.axis_index("dp")
        self.stages = chip_stages(lax.axis_size("seq") // 2)
        self.split = self.stages[0][0] if self.stages else 1
        self.digit = (self.seq // 2) % self.split
        self.rows = channels // (8 * self.split)
        self.channels = channels

    def row_order(self):
        p = jnp.arange(self.channels)
        inner = p % self.rows
        z = (p // self.rows) % self.split
        square = (p // (self.rows * self.split)) % 4
        pair = p // (self.rows * self.split * 4)
        rep, dp = self.rep ^ (square >> 1), self.dp ^ (square & 1)
        target = ((dp * 2 + (self.core ^ pair)) * 2 + rep) * self.split + (self.digit ^ z)
        target = target * self.rows + inner
        return (target[:, None] == jnp.arange(self.channels)[None, :]).astype(BF)


def gradient_kernel(width, has_proj, *refs):
    if has_proj:
        xm, xg, bm, bg, am, cm, cg, own, s1, s2, s3 = refs
    else:
        xm, xg, bm, bg, own, s1, s2, s3 = refs
    quarter = own.shape[0]
    tile = 384
    x_far = xg[xg.shape[0] - 4 * quarter :, :]

    def put(first, total):
        columns = slice(first, first + tile)
        own[:, columns] = total[:quarter]
        for k, ref in enumerate((s1, s2, s3)):
            ref[:, columns] = total[(k + 1) * quarter : (k + 2) * quarter].astype(BF)

    for first in range(0, width, tile):
        rows = slice(first, first + tile)
        total = lax.dot_general(xm[...], bm[rows, :], OVER_LANES, preferred_element_type=F32)
        put(first, total + lax.dot_general(x_far, bg[rows, :], OVER_LANES, preferred_element_type=F32))
    if has_proj:
        far = bg[width:, :]
        for first in range(0, cm.shape[1], tile):
            columns = slice(first, first + tile)
            total = jnp.dot(am[...], cm[:, columns], preferred_element_type=F32)
            put(width + first, total + jnp.dot(far, cg[:, columns], preferred_element_type=F32))


def chip_gradient(operands):
    rows, n = operands[0].shape
    width = operands[2].shape[0] - rows
    has_proj = len(operands) > 4
    total = width + (operands[5].shape[1] if has_proj else 0)
    vmem = pl.BlockSpec(memory_space=pltpu.VMEM)
    wire = jax.ShapeDtypeStruct((rows // 4, total), BF)
    return pl.pallas_call(
        functools.partial(gradient_kernel, width, has_proj),
        out_shape=(jax.ShapeDtypeStruct((rows // 4, total), F32), wire, wire, wire),
        in_specs=[vmem] * len(operands),
        out_specs=(vmem,) * 4,
        compiler_params=pltpu.CompilerParams(vmem_limit_bytes=60 * 1024 * 1024),
        cost_estimate=busy(1.5, 3.5),
        name="chip_gradient",
    )(*operands)


def sum_square(own, sends, place):
    got = [own] + [swapped(s, ("rep", "dp"), k + 1).astype(F32) for k, s in enumerate(sends)]
    return tree_sum(got)


def sum_chips(total, place, *others):
    parts = total.reshape(place.split, place.rows, -1)
    got = [parts[0]]
    for k in range(1, place.split):
        there = swapped(parts[k].astype(BF), "seq", 2 * k)
        got.append((after(there, *others) if others else there).astype(F32))
    total = tree_sum(got)
    for radix, stride in place.stages[1:]:
        held = total.astype(BF)
        got = [swapped(held, "seq", 2 * k * stride) if k else held for k in range(radix)]
        total = tree_sum([g.astype(F32) for g in got])
    return total.astype(BF)


def gather_blocks(block, place, *others):
    got = [swapped(block, "seq", 2 * k) if k else block for k in range(place.split)]
    if others:
        got[-1] = after(got[-1], *others)
    chips = jnp.concatenate(got)
    other_rep = swapped(chips, "rep", 1)
    return chips, other_rep, swapped(chips, "seq", 1), swapped(other_rep, "seq", 1)


def assemble_kernel(split, factor, group, at, *refs):
    first, second = refs[:4], refs[4:8]
    qkv, proj = refs[8], refs[9]
    rows = first[0].shape[0] // split
    third = qkv.shape[1] // 3
    rest = third - group
    for pair in range(2):
        for square in range(2):
            index = 2 * pair + square
            base = ((at[0] ^ pair) * 2 + (at[1] ^ square)) * split
            for z in range(split):
                here = slice(z * rows, (z + 1) * rows)
                there = pl.ds(pl.multiple_of((base + (at[2] ^ z)) * rows, rows), rows)
                for part in range(3):
                    low, mid = part * third, part * third + group
                    a = first[index][here, part * group : (part + 1) * group]
                    qkv[there, low:mid] = a.astype(F32) * factor
                    b = second[index][here, part * rest : (part + 1) * rest]
                    qkv[there, mid : low + third] = b.astype(F32) * factor
                proj[there, :] = second[index][here, 3 * rest :].astype(F32) * factor


def assemble(first, second, place, factor, group):
    rows = 4 * first[0].shape[0]
    channels = place.channels
    vmem = pl.BlockSpec(memory_space=pltpu.VMEM)
    smem = pl.BlockSpec(memory_space=pltpu.SMEM)
    at = jnp.stack([place.core, place.rep, place.digit]).astype(jnp.int32)
    return pl.pallas_call(
        functools.partial(assemble_kernel, place.split, factor, group),
        out_shape=(
            jax.ShapeDtypeStruct((rows, 3 * channels), F32),
            jax.ShapeDtypeStruct((rows, channels), F32),
        ),
        in_specs=[smem] + [vmem] * 8,
        out_specs=(vmem, vmem),
        compiler_params=pltpu.CompilerParams(vmem_limit_bytes=60 * 1024 * 1024),
        cost_estimate=busy(3, 7),
        name="assemble",
    )(at, *first, *second)


def sum_steps(x, place):
    half = x.shape[0] // 2
    low = place.core == 0
    x = jnp.where(low, x[:half], x[half:]) + swapped(
        jnp.where(low, x[half:], x[:half]), "seq", 1
    )
    x = x + swapped(x, "rep", 1)
    yield x
    x = x + swapped(x, "dp", 1)
    yield x
    flip = 2
    while flip < lax.axis_size("seq"):
        x = x + swapped(x, "seq", flip)
        yield x
        flip = flip * 2
    got = swapped(x, "seq", 1)
    yield jnp.concatenate([jnp.where(low, x, got), jnp.where(low, got, x)])


def rows_of_both(mine, got, other, place):
    half = got.shape[0]
    m0, m1 = mine[:half], mine[half:]
    p0 = jnp.where(place.core == 0, got, other)
    p1 = jnp.where(place.core == 0, other, got)
    low = place.dp == 0
    return jnp.concatenate(
        [jnp.where(low, a, b) for a, b in ((m0, p0), (m1, p1), (p0, m0), (p1, m1))]
    )


GROUP_HEADS = 16


def into_field(nums, mine, theirs):
    count = mine.shape[0] // HALF
    mine = mine.astype(F32).reshape(count, HALF, -1)
    theirs = theirs.astype(F32).reshape(count, HALF, -1)
    column = lax.broadcasted_iota(jnp.int32, mine.shape, 1)
    low = (column >= nums[1]).astype(jnp.int32) == nums[4]
    return jnp.concatenate([jnp.where(low, mine, theirs), jnp.where(low, theirs, mine)], axis=1)


def field_kernel(*refs):
    nums, back, att, got, mixed, unit, inverse, cot, padded, gain, scale = refs[:11]
    w_mine, w_got, w_other = refs[11:14]
    bm, inner, outer, out, small = refs[14:]
    depth, height, width, channels = mixed.shape
    half = back.shape[0]
    rows = depth * height
    restored = into_field(nums, att[...], got[half:, :]).reshape(rows * width, channels)
    low_rows, low_core = nums[3] == 0, nums[4] == 0
    side, part = channels // 2, channels // 4
    r_mine = jnp.where(low_rows, restored[:, :side], restored[:, side:]).astype(BF)
    r_peer = jnp.where(low_rows, restored[:, side:], restored[:, :side])
    r_got = jnp.where(low_core, r_peer[:, :part], r_peer[:, part:]).astype(BF)
    r_other = jnp.where(low_core, r_peer[:, part:], r_peer[:, :part]).astype(BF)
    projected = jnp.dot(r_mine, w_mine[...], preferred_element_type=F32)
    projected = projected + jnp.dot(r_got, w_got[:, :channels], preferred_element_type=F32)
    projected = projected + jnp.dot(r_other, w_other[:, :channels], preferred_element_type=F32)
    out[...] = (mixed[...] + projected.reshape(mixed.shape)).astype(BF)

    normed = into_field(nums, back[...], got[:half, :])
    field = unit[...].reshape(rows, width, channels)
    small[27:28, :] = jnp.sum(jnp.sum(normed * field, axis=0), axis=0, keepdims=True)
    grad = normed * gain[...].reshape(1, 1, channels)
    mean = jnp.mean(grad, axis=-1, keepdims=True)
    slope = jnp.mean(grad * field, axis=-1, keepdims=True)
    std = inverse[...].reshape(rows, width, 1)
    value = cot[...].astype(F32).reshape(rows, width, channels) + std * (grad - mean - field * slope)
    bm[...] = value.reshape(mixed.shape)
    first, last = value[:height].astype(BF), value[rows - height :].astype(BF)
    inner[...] = jnp.where(low_core, last.astype(F32), first.astype(F32)).astype(BF)
    outer[...] = jnp.where(low_core, first.astype(F32), last.astype(F32)).astype(BF)

    tile = 128
    for start in range(0, channels, tile):
        lanes = slice(start, start + tile)
        mixed_back = bm[:, :, :, lanes]
        for e in range(3):
            shifted = padded[:, :, e : e + width, lanes].astype(F32)
            for a in range(3):
                for b in range(3):
                    product = mixed_back * shifted[a : a + depth, b : b + height]
                    row = jnp.sum(jnp.sum(product, axis=(0, 1)), axis=0, keepdims=True)
                    small[9 * a + 3 * b + e : 9 * a + 3 * b + e + 1, lanes] = row
    sums = jnp.sum(scale[...], axis=1, keepdims=True)
    heads = sums.shape[0]
    same = lax.broadcasted_iota(jnp.int32, (heads, channels), 0) == lax.broadcasted_iota(
        jnp.int32, (heads, channels), 1
    )
    small[28:29, :] = jnp.sum(jnp.where(same, sums, 0.0), axis=0, keepdims=True)
    small[29:32, :] = jnp.zeros((3, channels), F32)


def field_back(operands):
    mixed = operands[4]
    vmem = pl.BlockSpec(memory_space=pltpu.VMEM)
    smem = pl.BlockSpec(memory_space=pltpu.SMEM)
    plane = jax.ShapeDtypeStruct(mixed.shape[1:], BF)
    return pl.pallas_call(
        field_kernel,
        out_shape=(
            jax.ShapeDtypeStruct(mixed.shape, F32),
            plane,
            plane,
            jax.ShapeDtypeStruct(mixed.shape, BF),
            jax.ShapeDtypeStruct((32, mixed.shape[-1]), F32),
        ),
        in_specs=[smem] + [vmem] * (len(operands) - 1),
        out_specs=(vmem,) * 5,
        compiler_params=pltpu.CompilerParams(vmem_limit_bytes=60 * 1024 * 1024),
        cost_estimate=busy(1, 2),
        name="field_back",
    )(*operands)


def per_device(tokens, cotangent, w_qkv, w_proj, conv_weight, norm_gain, head_scale, shift_offsets):
    slab = tokens[0]
    cot = cotangent[0]
    depth, height, width, channels = slab.shape
    head_count = head_scale.shape[0]
    head_dim = channels // head_count
    place = Place(channels)
    core, dp = place.core, place.dp
    rows_shift, cols_shift = shift_offsets[0], shift_offsets[1]
    positions = depth * height * width
    half = positions // 2
    columns = jnp.arange(HALF)[None, None, :, None]
    straight = (columns >= cols_shift) == (core == 1)
    group = GROUP_HEADS * head_dim

    def split_columns(field):
        low, high = field[:, :, :HALF], field[:, :, HALF:]
        return (
            jnp.where(straight, low, high).reshape(half, -1),
            jnp.where(straight, high, low).reshape(half, -1),
        )

    def join_columns(mine, theirs):
        mine = mine.reshape(depth, height, HALF, -1)
        theirs = theirs.reshape(depth, height, HALF, -1)
        return jnp.concatenate(
            [jnp.where(straight, mine, theirs), jnp.where(straight, theirs, mine)], axis=2
        )

    spatial = ((0, 0), (1, 1), (1, 1), (0, 0))
    weights_part, inner, outer = stage(core, w_qkv, w_proj, tokens)
    outer = edge_partner(outer)
    inner = swapped(inner, "seq", 1)
    weights_got = swapped(weights_part, "dp", 1)
    cot_mine, cot_theirs = split_columns(cot)
    cot_got = window_partner(cot_theirs)
    padded_tokens = jnp.pad(with_halo(slab, inner, after(outer, cot_got), core), spatial)
    cot_window = jnp.concatenate([cot_mine, cot_got])
    order = place.row_order()

    mixed_field = slab.astype(F32) + tap_sum(
        padded_tokens, conv_weight, depth, height, width, False
    )
    centred = mixed_field - jnp.mean(mixed_field, axis=-1, keepdims=True)
    inverse_std = lax.rsqrt(jnp.mean(centred * centred, axis=-1, keepdims=True) + 1e-05)
    unit_field = centred * inverse_std
    normed = (unit_field * norm_gain).astype(BF)
    x_mine, x_theirs = split_columns(normed)
    x_theirs = window_partner(x_theirs)
    weights_got = after(weights_got, x_theirs)
    weights_other = swapped(weights_got, "seq", 1)
    cot_other = swapped(cot_window, "seq", 1)
    nums = jnp.stack([rows_shift, cols_shift, 1 - core, dp, core]).astype(jnp.int32)
    half_rows = channels // 2
    send_first, x_rows, att_first, back_attended, scale_first = attention_call(
        first_kernel,
        "first_heads",
        group,
        head_dim,
        head_count,
        (3 * group + half_rows, half_rows, group, channels),
        (nums, head_scale, x_mine, x_theirs, cot_window, order, w_qkv, w_proj, weights_got, weights_other),
    )
    got_first = swapped(send_first, "seq", 1)
    own, *sends = chip_gradient((x_rows, got_first, send_first, got_first))
    rest = channels - group
    send_second, att_rows, att_second, scale_second = attention_call(
        second_kernel,
        "second_heads",
        rest,
        head_dim,
        head_count,
        (3 * rest + half_rows, half_rows, rest),
        (
            nums,
            head_scale,
            x_mine,
            x_theirs,
            order,
            w_qkv,
            weights_got,
            weights_other,
            after(back_attended, own),
            att_first,
        ),
    )
    first_own, first_sends = own, sends

    got_second = swapped(send_second, "seq", 1)
    back_mine, window_send, att_mine = back_through(
        group,
        (
            nums,
            send_first,
            send_second,
            w_qkv,
            weights_got,
            weights_other,
            att_first,
            att_second,
        ),
    )
    first_total = sum_square(first_own, first_sends, place)
    own, *sends = chip_gradient(
        (
            after(x_rows, back_mine, first_total),
            got_first,
            send_second,
            got_second,
            att_rows,
            cot_window,
            cot_other,
        )
    )
    window_got = after(window_partner(window_send), own)
    scale_rows = jnp.concatenate([scale_first, scale_second])
    back_mixed, inner, outer, output, small = field_back(
        (
            nums,
            back_mine,
            att_mine,
            window_got,
            mixed_field,
            unit_field,
            inverse_std,
            cot,
            padded_tokens,
            norm_gain[None],
            scale_rows,
            w_proj,
            weights_got,
            weights_other,
        )
    )
    second_total = sum_square(after(own, small), sends, place)
    first_block = sum_chips(first_total, place, second_total)
    steps = sum_steps(after(small, second_total), place)
    small = next(steps)
    small = next(steps)
    second_block = sum_chips(second_total, place)
    small = next(steps)
    factor = 1.0 / math.sqrt(
        lax.axis_size("rep") * lax.axis_size("dp") * lax.axis_size("seq") * positions
    )
    grad_qkv, grad_proj = assemble(
        gather_blocks(first_block, place), gather_blocks(second_block, place, small), place, factor, group
    )
    inner = swapped(after(inner, second_total), "seq", 1)
    outer = edge_partner(after(outer, second_total))
    padded_back = jnp.pad(
        with_halo(back_mixed, inner.astype(F32), outer.astype(F32), core), spatial
    )
    grad_tokens = (
        back_mixed + tap_sum(padded_back, conv_weight, depth, height, width, True)
    ).astype(BF)
    for small in steps:
        pass
    small = small * factor
    taps = conv_weight.shape[0]
    return (
        output[None],
        grad_tokens[None],
        grad_qkv,
        grad_proj,
        small[:taps],
        small[taps],
        small[taps + 1, :head_count],
    )


def solution(mesh):
    block = P(("rep", "dp"), "seq", None, None, None)
    rows = P("dp", None)
    return jax.shard_map(
        per_device,
        mesh=mesh,
        in_specs=(block, block, rows, rows, P(), P(), P(), P()),
        out_specs=(block, block, rows, rows, P(), P(), P()),
        check_vma=False,
    )
```

```python
import functools
import math

import jax
import jax.numpy as jnp
from jax import lax
from jax.experimental import pallas as pl
from jax.experimental.pallas import tpu as pltpu
from jax.sharding import PartitionSpec as P

HALF = 8
LOG2_E = math.log2(math.e)
BF = jnp.bfloat16
F32 = jnp.float32


def busy(microseconds, megabytes):
    return pl.CostEstimate(
        flops=int(microseconds * 0.5e7), bytes_accessed=int(megabytes * 0.1e6), transcendentals=0
    )


def swapped(x, axis, flip):
    count = 1
    for name in (axis,) if isinstance(axis, str) else axis:
        count = count * lax.axis_size(name)
    return lax.ppermute(x, axis, [(i, i ^ flip) for i in range(count)])


def window_partner(x):
    count = lax.axis_size("seq")
    pairs = [(i, (i + 1) % count if i % 2 else (i - 1) % count) for i in range(count)]
    return lax.ppermute(x, "seq", pairs)


def edge_partner(x):
    count = lax.axis_size("seq")
    pairs = [(i, i + 1) for i in range(1, count - 1, 2)]
    return lax.ppermute(x, "seq", pairs + [(j, i) for i, j in pairs])


def with_halo(x, inner, outer, core):
    low = core == 0
    return jnp.concatenate(
        [jnp.where(low, outer, inner)[None], x, jnp.where(low, inner, outer)[None]], axis=0
    )


def tap_sum(padded, weight, slab_depth, height, grid_width, flipped):
    summed = jnp.zeros((slab_depth, height, grid_width, padded.shape[-1]), F32)
    for a in range(3):
        for b in range(3):
            for e in range(3):
                starts = (2 - a, 2 - b, 2 - e) if flipped else (a, b, e)
                part = padded[
                    starts[0] : starts[0] + slab_depth,
                    starts[1] : starts[1] + height,
                    starts[2] : starts[2] + grid_width,
                ]
                summed = summed + weight[9 * a + 3 * b + e] * part.astype(F32)
    return summed


OVER_ROWS = (((0,), (0,)), ((), ()))
OVER_LANES = (((1,), (1,)), ((), ()))


def allowed_pairs(nums, n):
    rows_shift, cols_shift, second = nums[0], nums[1], nums[2]

    def code(dim):
        t = lax.broadcasted_iota(jnp.int32, (n, n), dim)
        first_bit = jnp.where(((t >> 3) & 7) < rows_shift, 2, 0)
        return first_bit + jnp.where((t & 7) < cols_shift, second, 0)

    return jnp.where(code(0) == code(1), 1.0, 0.0).astype(F32)


def project(nums, x, mine, got, other, group, qkv):
    channels = x.shape[1]
    half = channels // 2
    quarter = half // 2
    low_rows, low_core = nums[3] == 0, nums[4] == 0
    x = x.astype(F32)
    x_mine = jnp.where(low_rows, x[:, :half], x[:, half:])
    x_peer = jnp.where(low_rows, x[:, half:], x[:, :half])
    x_got = jnp.where(low_core, x_peer[:, :quarter], x_peer[:, quarter:]).astype(BF)
    x_other = jnp.where(low_core, x_peer[:, quarter:], x_peer[:, :quarter]).astype(BF)
    x_mine = x_mine.astype(BF)
    for part in range(3):
        total = jnp.dot(x_mine, mine(part), preferred_element_type=F32)
        total = total + jnp.dot(x_got, got(part), preferred_element_type=F32)
        total = total + jnp.dot(x_other, other(part), preferred_element_type=F32)
        qkv[part * group : (part + 1) * group, :] = total.T.astype(BF)


def attend(head_dim, allowed, scale, base, group, qkv, ba, ba_low, att, back, gs):
    def unit(raw):
        inverse = lax.rsqrt(jnp.sum(raw * raw, axis=0, keepdims=True) + 1.0)
        return inverse, (raw * inverse).astype(BF)

    def radius_back(raw, inverse, grad):
        inner = jnp.sum(raw * grad, axis=0, keepdims=True)
        return grad * inverse - raw * (inner * (inverse * inverse * inverse))

    def one_head(h):
        def rows(start):
            return pl.ds(pl.multiple_of(start + h * head_dim, head_dim), head_dim)

        s = scale[base + h]
        qf = qkv[rows(0), :].astype(F32)
        kf = qkv[rows(group), :].astype(F32)
        v = qkv[rows(2 * group), :]
        b = ba[rows(ba_low), :]
        iq, uq = unit(qf)
        ik, uk = unit(kf)
        cosine = lax.dot_general(uk, uq, OVER_ROWS, preferred_element_type=F32)
        back_prob = lax.dot_general(v, b, OVER_ROWS, preferred_element_type=F32)
        expo = jnp.exp2(cosine * (s * LOG2_E)) * allowed
        inverse = 1.0 / jnp.sum(expo, axis=0, keepdims=True)
        weights = (expo * inverse).astype(BF)
        att[rows(0), :] = jnp.dot(v, weights, preferred_element_type=F32).astype(BF)
        mean = jnp.sum(expo * back_prob, axis=0, keepdims=True) * inverse
        scaled = expo * (inverse * s) * (back_prob - mean)
        gs[pl.ds(h, 1), :] = jnp.sum(scaled * cosine, axis=0, keepdims=True) * (1.0 / s)
        scaled = scaled.astype(BF)
        buq = jnp.dot(uk, scaled, preferred_element_type=F32)
        buk = lax.dot_general(uq, scaled, OVER_LANES, preferred_element_type=F32)
        bv = lax.dot_general(b, weights, OVER_LANES, preferred_element_type=F32)
        back[rows(0), :] = radius_back(qf, iq, buq).astype(BF)
        back[rows(group), :] = radius_back(kf, ik, buk).astype(BF)
        back[rows(2 * group), :] = bv.astype(BF)

    count = group // head_dim
    unrolled = math.gcd(count, 10) if count > 8 else count

    def body(i, carry):
        for u in range(unrolled):
            one_head(i * unrolled + u)
        return carry

    lax.fori_loop(0, count // unrolled, body, 0)


def first_kernel(group, head_dim, nums, scale, xm, xg, cot, w_qkv, w_proj, got, other, *outs):
    send, att, ba, gs, qkv = outs
    channels = xm.shape[1]
    half = channels // 2
    x = jnp.concatenate([xm[...], xg[...]], axis=0)

    def columns(ref, base):
        return lambda part: ref[:, base + part * channels : base + part * channels + group]

    far = (columns(got, channels), columns(other, channels))
    project(nums, x, columns(w_qkv, 0), *far, group, qkv)
    quarter = half // 2
    dp, core = nums[3], nums[4]

    def back_rows(start, count, weight):
        value = lax.dot_general(weight, cot[...], OVER_LANES, preferred_element_type=F32)
        ba[pl.ds(pl.multiple_of(start, quarter), count), :] = value.astype(BF)

    back_rows(dp * half, half, w_proj[...])
    back_rows((1 - dp) * half + core * quarter, quarter, got[:, :channels])
    back_rows((1 - dp) * half + (1 - core) * quarter, quarter, other[:, :channels])
    allowed = allowed_pairs(nums, x.shape[0])
    attend(head_dim, allowed, scale, 0, group, qkv, ba, 0, att, send, gs)


def second_kernel(group, head_dim, nums, scale, xm, xg, order, ba, att_first, *refs):
    weights, (send, att_rows, att, gs, qkv) = refs[:9], refs[9:]
    channels = xm.shape[1]
    half = channels // 2
    low = channels - group
    x = jnp.concatenate([xm[...], xg[...]], axis=0)
    mine, got, other = [lambda part, refs=weights[i : i + 3]: refs[part][...] for i in (0, 3, 6)]
    project(nums, x, mine, got, other, group, qkv)
    allowed = allowed_pairs(nums, x.shape[0])
    attend(head_dim, allowed, scale, low // head_dim, group, qkv, ba, low, att, send, gs)

    def ordered(rows):
        total = jnp.dot(order[rows, :low], att_first[...], preferred_element_type=F32)
        total = total + jnp.dot(order[rows, low:], att[...], preferred_element_type=F32)
        return total.astype(BF)

    att_rows[...] = ordered(slice(0, half))
    send[3 * group :, :] = ordered(slice(half, channels))


def attention_call(body, name, group, head_dim, head_count, outs, operands, columns=()):
    n = 2 * operands[2].shape[0]
    channels = operands[2].shape[1]
    vmem = pl.BlockSpec(memory_space=pltpu.VMEM)
    smem = pl.BlockSpec(memory_space=pltpu.SMEM)
    tail = operands[len(operands) - len(columns) :]
    blocks = [
        pl.BlockSpec((x.shape[0], wide), lambda i, at=at: (0, at)) for x, (wide, at) in zip(tail, columns)
    ]
    shapes = tuple(jax.ShapeDtypeStruct((rows, n), BF) for rows in outs)
    shapes = shapes + (jax.ShapeDtypeStruct((group // head_dim, n), F32),)
    return pl.pallas_call(
        functools.partial(body, group, head_dim),
        grid=(1,),
        out_shape=shapes,
        in_specs=[smem, smem] + [vmem] * (len(operands) - 2 - len(columns)) + blocks,
        out_specs=(vmem,) * len(shapes),
        scratch_shapes=[pltpu.VMEM((3 * group, n), BF)],
        compiler_params=pltpu.CompilerParams(vmem_limit_bytes=(60 if columns else 24) * 1024 * 1024),
        cost_estimate=busy(5 + 0.5 * (group // head_dim), 8),
        name=name,
    )(*operands)


def stage_kernel(core, w_qkv, w_proj, tokens, weights, inner, outer, sems):
    rows, channels = weights.shape[0], w_proj.shape[1]
    mine = pl.ds(pl.multiple_of(core[0] * rows, rows), rows)
    copies = (
        (w_proj.at[mine, :], weights.at[:, :channels]),
        (w_qkv.at[mine, :], weights.at[:, channels:]),
        (tokens.at[0, core[0]], outer),
        (tokens.at[0, 1 - core[0]], inner),
    )
    started = [pltpu.make_async_copy(x, y, sems.at[i]) for i, (x, y) in enumerate(copies)]
    for copy in started:
        copy.start()
    for copy in started:
        copy.wait()


def stage(core, w_qkv, w_proj, tokens):
    channels = w_proj.shape[1]
    rows = w_proj.shape[0] // 2
    anywhere = pl.BlockSpec(memory_space=pl.ANY)
    vmem = pl.BlockSpec(memory_space=pltpu.VMEM)
    plane = jax.ShapeDtypeStruct(tokens.shape[2:], BF)
    return pl.pallas_call(
        stage_kernel,
        out_shape=(jax.ShapeDtypeStruct((rows, 4 * channels), BF), plane, plane),
        in_specs=[pl.BlockSpec(memory_space=pltpu.SMEM)] + [anywhere] * 3,
        out_specs=(vmem,) * 3,
        scratch_shapes=[pltpu.SemaphoreType.DMA((4,))],
        cost_estimate=busy(2.5, 4),
        name="stage",
    )(core[None].astype(jnp.int32), w_qkv, w_proj, tokens)


def back_kernel(group, nums, first, second, w_qkv, got, other, att1, att2, *outs):
    mine, send, att_mine = outs
    n = first.shape[1]
    half = n // 2
    channels = att_mine.shape[1]
    rest = channels - group
    low_rows, low_core = nums[3] == 0, nums[4] == 0
    first_t = first[: 3 * group, :].astype(F32).T.astype(BF)
    second_t = second[: 3 * rest, :].astype(F32).T.astype(BF)

    def through(pieces):
        total = None
        for left, right in pieces:
            term = lax.dot_general(left, right, OVER_LANES, preferred_element_type=F32)
            total = term if total is None else total + term
        return total

    def pieces(weight, base):
        for part in range(3):
            low = base + part * channels
            yield first_t[:, part * group : (part + 1) * group], weight[:, low : low + group]
            yield second_t[:, part * rest : (part + 1) * rest], weight[:, low + group : low + channels]

    from_mine = through(pieces(w_qkv, 0))
    from_got = through(pieces(got, channels))
    from_other = through(pieces(other, channels))
    from_peer = jnp.concatenate(
        [jnp.where(low_core, from_got, from_other), jnp.where(low_core, from_other, from_got)], axis=1
    )
    shifted = jnp.concatenate(
        [jnp.where(low_rows, from_mine, from_peer), jnp.where(low_rows, from_peer, from_mine)], axis=1
    ).astype(BF)
    mine[...] = shifted[:half]
    send[:half, :] = shifted[half:]
    for low, ref in ((0, att1), (group, att2)):
        wide = slice(low, low + ref.shape[0])
        turned = ref[...].astype(F32).T.astype(BF)
        att_mine[:, wide] = turned[:half]
        send[half:, wide] = turned[half:]


def back_through(group, operands):
    n = operands[1].shape[1]
    channels = operands[6].shape[0] + operands[7].shape[0]
    vmem = pl.BlockSpec(memory_space=pltpu.VMEM)
    smem = pl.BlockSpec(memory_space=pltpu.SMEM)
    half = jax.ShapeDtypeStruct((n // 2, channels), BF)
    return pl.pallas_call(
        functools.partial(back_kernel, group),
        out_shape=(half, jax.ShapeDtypeStruct((n, channels), BF), half),
        in_specs=[smem] + [vmem] * (len(operands) - 1),
        out_specs=(vmem,) * 3,
        compiler_params=pltpu.CompilerParams(vmem_limit_bytes=60 * 1024 * 1024),
        cost_estimate=busy(4, 8),
        name="back_through",
    )(*operands)


def after(x, *others):
    anywhere = pl.BlockSpec(memory_space=pl.ANY)

    def nothing(*refs):
        del refs

    return pl.pallas_call(
        nothing,
        out_shape=jax.ShapeDtypeStruct(x.shape, x.dtype),
        in_specs=[anywhere] * (1 + len(others)),
        out_specs=anywhere,
        input_output_aliases={0: 0},
        name="ordered",
    )(x, *others)


def pick(x, index, axis):
    return lax.dynamic_index_in_dim(x, index, axis, keepdims=False)


def tree_sum(parts):
    while len(parts) > 1:
        parts = [a + b for a, b in zip(parts[::2], parts[1::2])]
    return parts[0]


def chip_stages(chips):
    stages = []
    stride = 1
    while stride < chips:
        radix = 4 if (chips // stride) % 4 == 0 else 2
        stages.append((radix, stride))
        stride = stride * radix
    return stages


class Place:
    def __init__(self, channels):
        self.seq = lax.axis_index("seq")
        self.core = self.seq % 2
        self.rep, self.dp = lax.axis_index("rep"), lax.axis_index("dp")
        self.stages = chip_stages(lax.axis_size("seq") // 2)
        self.split = self.stages[0][0] if self.stages else 1
        self.digit = (self.seq // 2) % self.split
        self.rows = channels // (8 * self.split)
        self.channels = channels

    def row_order(self):
        p = jnp.arange(self.channels)
        inner = p % self.rows
        z = (p // self.rows) % self.split
        square = (p // (self.rows * self.split)) % 4
        pair = p // (self.rows * self.split * 4)
        rep, dp = self.rep ^ (square >> 1), self.dp ^ (square & 1)
        target = ((dp * 2 + (self.core ^ pair)) * 2 + rep) * self.split + (self.digit ^ z)
        target = target * self.rows + inner
        return (target[:, None] == jnp.arange(self.channels)[None, :]).astype(BF)


def gradient_kernel(width, has_proj, *refs):
    if has_proj:
        xm, xg, bm, bg, am, cm, cg, own, s1, s2, s3 = refs
    else:
        xm, xg, bm, bg, own, s1, s2, s3 = refs
    quarter = own.shape[0]
    tile = 384
    x_far = xg[...]

    def put(first, total):
        columns = slice(first, first + tile)
        own[:, columns] = total[:quarter]
        for k, ref in enumerate((s1, s2, s3)):
            ref[:, columns] = total[(k + 1) * quarter : (k + 2) * quarter].astype(BF)

    for first in range(0, width, tile):
        rows = slice(first, first + tile)
        total = lax.dot_general(xm[...], bm[rows, :], OVER_LANES, preferred_element_type=F32)
        put(first, total + lax.dot_general(x_far, bg[rows, :], OVER_LANES, preferred_element_type=F32))
    if has_proj:
        far = bg[width:, :]
        for first in range(0, cm.shape[1], tile):
            columns = slice(first, first + tile)
            total = jnp.dot(am[...], cm[:, columns], preferred_element_type=F32)
            put(width + first, total + jnp.dot(far, cg[:, columns], preferred_element_type=F32))


def chip_gradient(group, operands):
    rows, n = operands[0].shape
    width = 3 * group
    has_proj = len(operands) > 4
    total = width + (operands[5].shape[1] if has_proj else 0)
    vmem = pl.BlockSpec(memory_space=pltpu.VMEM)
    wire = jax.ShapeDtypeStruct((rows // 4, total), BF)
    return pl.pallas_call(
        functools.partial(gradient_kernel, width, has_proj),
        out_shape=(jax.ShapeDtypeStruct((rows // 4, total), F32), wire, wire, wire),
        in_specs=[vmem] * len(operands),
        out_specs=(vmem,) * 4,
        compiler_params=pltpu.CompilerParams(vmem_limit_bytes=12 * 1024 * 1024),
        cost_estimate=busy(1.5, 3.5),
        name="chip_gradient",
    )(*operands)


def sum_square(own, sends, place):
    got = [own] + [swapped(s, ("rep", "dp"), k + 1).astype(F32) for k, s in enumerate(sends)]
    return tree_sum(got)


def sum_chips(total, place, *others):
    parts = total.reshape(place.split, place.rows, -1)
    got = [parts[0]]
    for k in range(1, place.split):
        there = swapped(parts[k].astype(BF), "seq", 2 * k)
        got.append((after(there, *others) if others and k == 1 else there).astype(F32))
    total = tree_sum(got)
    for radix, stride in place.stages[1:]:
        held = total.astype(BF)
        got = [swapped(held, "seq", 2 * k * stride) if k else held for k in range(radix)]
        total = tree_sum([g.astype(F32) for g in got])
    return total.astype(BF)


def gather_blocks(block, place, *others):
    got = [swapped(block, "seq", 2 * k) if k else block for k in range(place.split)]
    if others:
        got[-1] = after(got[-1], *others)
    chips = jnp.concatenate(got)
    other_rep = swapped(chips, "rep", 1)
    return chips, other_rep, swapped(chips, "seq", 1), swapped(other_rep, "seq", 1)


def assemble_kernel(split, factor, group, at, *refs):
    first, second = refs[:4], refs[4:8]
    qkv, proj = refs[8], refs[9]
    rows = first[0].shape[0] // split
    third = qkv.shape[1] // 3
    rest = third - group
    for pair in range(2):
        for square in range(2):
            index = 2 * pair + square
            base = ((at[4] ^ pair) * 2 + (at[5] ^ square)) * split
            for z in range(split):
                here = slice(z * rows, (z + 1) * rows)
                there = pl.ds(pl.multiple_of((base + (at[6] ^ z)) * rows, rows), rows)
                for part in range(3):
                    low, mid = part * third, part * third + group
                    a = first[index][here, part * group : (part + 1) * group]
                    qkv[there, low:mid] = a.astype(F32) * factor
                    b = second[index][here, part * rest : (part + 1) * rest]
                    qkv[there, mid : low + third] = b.astype(F32) * factor
                proj[there, :] = second[index][here, 3 * rest :].astype(F32) * factor


def assemble(nums, first, second, place, factor, group):
    rows = 4 * first[0].shape[0]
    channels = place.channels
    vmem = pl.BlockSpec(memory_space=pltpu.VMEM)
    smem = pl.BlockSpec(memory_space=pltpu.SMEM)
    return pl.pallas_call(
        functools.partial(assemble_kernel, place.split, factor, group),
        out_shape=(
            jax.ShapeDtypeStruct((rows, 3 * channels), F32),
            jax.ShapeDtypeStruct((rows, channels), F32),
        ),
        in_specs=[smem] + [vmem] * 8,
        out_specs=(vmem, vmem),
        compiler_params=pltpu.CompilerParams(vmem_limit_bytes=16 * 1024 * 1024),
        cost_estimate=busy(3, 7),
        name="assemble",
    )(nums, *first, *second)


def sum_steps(x, place):
    half = x.shape[0] // 2
    low = place.core == 0
    x = jnp.where(low, x[:half], x[half:]) + swapped(
        jnp.where(low, x[half:], x[:half]), "seq", 1
    )
    x = x + swapped(x, "rep", 1)
    yield x
    x = x + swapped(x, "dp", 1)
    yield x
    flip = 2
    while flip < lax.axis_size("seq"):
        x = x + swapped(x, "seq", flip)
        yield x
        flip = flip * 2
    got = swapped(x, "seq", 1)
    yield jnp.concatenate([jnp.where(low, x, got), jnp.where(low, got, x)])


def rows_of_both(mine, got, other, place):
    half = got.shape[0]
    m0, m1 = mine[:half], mine[half:]
    p0 = jnp.where(place.core == 0, got, other)
    p1 = jnp.where(place.core == 0, other, got)
    low = place.dp == 0
    return jnp.concatenate(
        [jnp.where(low, a, b) for a, b in ((m0, p0), (m1, p1), (p0, m0), (p1, m1))]
    )


GROUP_HEADS = 20


def into_field(nums, mine, theirs):
    count = mine.shape[0] // HALF
    mine = mine.astype(F32).reshape(count, HALF, -1)
    theirs = theirs.astype(F32).reshape(count, HALF, -1)
    column = lax.broadcasted_iota(jnp.int32, mine.shape, 1)
    low = (column >= nums[1]).astype(jnp.int32) == nums[4]
    return jnp.concatenate([jnp.where(low, mine, theirs), jnp.where(low, theirs, mine)], axis=1)


def field_kernel(*refs):
    nums, back, att, got, mixed, cot, padded, gain, scale1, scale2 = refs[:10]
    w_mine, w_got, w_other = refs[10:13]
    bm, inner, outer, out, small = refs[13:]
    depth, height, width, channels = mixed.shape
    half = back.shape[0]
    rows = depth * height
    restored = into_field(nums, att[...], got[half:, :]).reshape(rows * width, channels)
    low_rows, low_core = nums[3] == 0, nums[4] == 0
    side, part = channels // 2, channels // 4
    r_mine = jnp.where(low_rows, restored[:, :side], restored[:, side:]).astype(BF)
    r_peer = jnp.where(low_rows, restored[:, side:], restored[:, :side])
    r_got = jnp.where(low_core, r_peer[:, :part], r_peer[:, part:]).astype(BF)
    r_other = jnp.where(low_core, r_peer[:, part:], r_peer[:, :part]).astype(BF)
    projected = jnp.dot(r_mine, w_mine[...], preferred_element_type=F32)
    projected = projected + jnp.dot(r_got, w_got[...], preferred_element_type=F32)
    projected = projected + jnp.dot(r_other, w_other[...], preferred_element_type=F32)
    out[...] = (mixed[...] + projected.reshape(mixed.shape)).astype(BF)

    normed = into_field(nums, back[...], got[:half, :])
    field = mixed[...].reshape(rows, width, channels)
    field = field - jnp.mean(field, axis=-1, keepdims=True)
    std = lax.rsqrt(jnp.mean(field * field, axis=-1, keepdims=True) + 1e-05)
    field = field * std
    small[27:28, :] = jnp.sum(jnp.sum(normed * field, axis=0), axis=0, keepdims=True)
    grad = normed * gain[...].reshape(1, 1, channels)
    mean = jnp.mean(grad, axis=-1, keepdims=True)
    slope = jnp.mean(grad * field, axis=-1, keepdims=True)
    value = cot[...].astype(F32).reshape(rows, width, channels) + std * (grad - mean - field * slope)
    bm[...] = value.reshape(mixed.shape)
    first, last = value[:height].astype(BF), value[rows - height :].astype(BF)
    inner[...] = jnp.where(low_core, last.astype(F32), first.astype(F32)).astype(BF)
    outer[...] = jnp.where(low_core, first.astype(F32), last.astype(F32)).astype(BF)

    tile = 128
    for start in range(0, channels, tile):
        lanes = slice(start, start + tile)
        mixed_back = bm[:, :, :, lanes]
        for e in range(3):
            shifted = padded[:, :, e : e + width, lanes].astype(F32)
            for a in range(3):
                for b in range(3):
                    product = mixed_back * shifted[a : a + depth, b : b + height]
                    row = jnp.sum(jnp.sum(product, axis=(0, 1)), axis=0, keepdims=True)
                    small[9 * a + 3 * b + e : 9 * a + 3 * b + e + 1, lanes] = row
    sums = jnp.concatenate([scale1[...], scale2[...]], axis=0)
    sums = jnp.sum(sums, axis=1, keepdims=True)
    heads = sums.shape[0]
    same = lax.broadcasted_iota(jnp.int32, (heads, channels), 0) == lax.broadcasted_iota(
        jnp.int32, (heads, channels), 1
    )
    small[28:29, :] = jnp.sum(jnp.where(same, sums, 0.0), axis=0, keepdims=True)
    small[29:32, :] = jnp.zeros((3, channels), F32)


def field_back(operands):
    mixed = operands[4]
    channels = mixed.shape[-1]
    first_columns = pl.BlockSpec((operands[-1].shape[0], channels), lambda i: (0, 0))
    vmem = pl.BlockSpec(memory_space=pltpu.VMEM)
    smem = pl.BlockSpec(memory_space=pltpu.SMEM)
    plane = jax.ShapeDtypeStruct(mixed.shape[1:], BF)
    return pl.pallas_call(
        field_kernel,
        grid=(1,),
        out_shape=(
            jax.ShapeDtypeStruct(mixed.shape, F32),
            plane,
            plane,
            jax.ShapeDtypeStruct(mixed.shape, BF),
            jax.ShapeDtypeStruct((32, mixed.shape[-1]), F32),
        ),
        in_specs=[smem] + [vmem] * (len(operands) - 3) + [first_columns] * 2,
        out_specs=(vmem,) * 5,
        compiler_params=pltpu.CompilerParams(vmem_limit_bytes=60 * 1024 * 1024),
        cost_estimate=busy(1, 2),
        name="field_back",
    )(*operands)


def per_device(tokens, cotangent, w_qkv, w_proj, conv_weight, norm_gain, head_scale, shift_offsets):
    slab = tokens[0]
    cot = cotangent[0]
    depth, height, width, channels = slab.shape
    head_count = head_scale.shape[0]
    head_dim = channels // head_count
    place = Place(channels)
    core, dp = place.core, place.dp
    rows_shift, cols_shift = shift_offsets[0], shift_offsets[1]
    positions = depth * height * width
    half = positions // 2
    columns = jnp.arange(HALF)[None, None, :, None]
    straight = (columns >= cols_shift) == (core == 1)
    group = GROUP_HEADS * head_dim

    def split_columns(field):
        low, high = field[:, :, :HALF], field[:, :, HALF:]
        return (
            jnp.where(straight, low, high).reshape(half, -1),
            jnp.where(straight, high, low).reshape(half, -1),
        )

    def join_columns(mine, theirs):
        mine = mine.reshape(depth, height, HALF, -1)
        theirs = theirs.reshape(depth, height, HALF, -1)
        return jnp.concatenate(
            [jnp.where(straight, mine, theirs), jnp.where(straight, theirs, mine)], axis=2
        )

    spatial = ((0, 0), (1, 1), (1, 1), (0, 0))
    weights_part, inner, outer = stage(core, w_qkv, w_proj, tokens)
    outer = edge_partner(outer)
    inner = swapped(inner, "seq", 1)
    weights_got = swapped(weights_part, "dp", 1)
    cot_mine, cot_theirs = split_columns(cot)
    cot_got = window_partner(cot_theirs)
    padded_tokens = jnp.pad(with_halo(slab, inner, after(outer, cot_got), core), spatial)
    cot_window = jnp.concatenate([cot_mine, cot_got])
    order = after(place.row_order(), cot_got)

    mixed_field = slab.astype(F32) + tap_sum(
        padded_tokens, conv_weight, depth, height, width, False
    )
    centred = mixed_field - jnp.mean(mixed_field, axis=-1, keepdims=True)
    inverse_std = lax.rsqrt(jnp.mean(centred * centred, axis=-1, keepdims=True) + 1e-05)
    unit_field = centred * inverse_std
    normed = (unit_field * norm_gain).astype(BF)
    x_mine, x_theirs = split_columns(normed)
    x_theirs = window_partner(x_theirs)
    x_rows = jnp.einsum(
        "pc,tc->pt",
        order,
        jnp.concatenate([x_mine, x_theirs]),
        preferred_element_type=F32,
    ).astype(BF)
    x_other = swapped(x_rows[channels // 2 :], "seq", 1)
    x_rows = x_rows[: channels // 2]
    weights_got = after(weights_got, x_other)
    weights_other = swapped(weights_got, "seq", 1)
    cot_other = swapped(cot_window, "seq", 1)
    nums = jnp.stack(
        [rows_shift, cols_shift, 1 - core, dp, core, place.rep, place.digit]
    ).astype(jnp.int32)
    half_rows = channels // 2
    send_first, att_first, back_attended, scale_first = attention_call(
        first_kernel,
        "first_heads",
        group,
        head_dim,
        head_count,
        (3 * group, group, channels),
        (nums, head_scale, x_mine, x_theirs, cot_window, w_qkv, w_proj, weights_got, weights_other),
    )
    got_first = swapped(send_first, "seq", 1)
    own, *sends = chip_gradient(group, (x_rows, x_other, send_first, got_first))
    rest = channels - group
    parts = [part * channels + group for part in range(3)]
    send_second, att_rows, att_second, scale_second = attention_call(
        second_kernel,
        "second_heads",
        rest,
        head_dim,
        head_count,
        (3 * rest + half_rows, half_rows, rest),
        (
            nums,
            head_scale,
            x_mine,
            x_theirs,
            order,
            after(back_attended, own),
            att_first,
            *[w_qkv] * 3,
            *[weights_got] * 3,
            *[weights_other] * 3,
        ),
        [(rest, base // rest) for base in parts]
        + [(rest, (base + channels) // rest) for base in parts] * 2,
    )
    first_own, first_sends = own, sends

    got_second = swapped(send_second, "seq", 1)
    back_mine, window_send, att_mine = back_through(
        group,
        (
            nums,
            send_first,
            send_second,
            w_qkv,
            weights_got,
            weights_other,
            att_first,
            att_second,
        ),
    )
    first_total = sum_square(first_own, first_sends, place)
    own, *sends = chip_gradient(
        rest,
        (
            after(x_rows, back_mine, first_total),
            x_other,
            send_second,
            got_second,
            att_rows,
            cot_window,
            cot_other,
        )
    )
    window_got = after(window_partner(window_send), own)
    back_mixed, inner, outer, output, small = field_back(
        (
            nums,
            back_mine,
            att_mine,
            window_got,
            mixed_field,
            cot,
            padded_tokens,
            norm_gain,
            scale_first,
            scale_second,
            w_proj,
            weights_got,
            weights_other,
        )
    )
    second_total = sum_square(after(own, small), sends, place)
    first_block = sum_chips(first_total, place, second_total)
    steps = sum_steps(after(small, second_total), place)
    small = next(steps)
    small = next(steps)
    second_block = sum_chips(second_total, place)
    small = next(steps)
    factor = 1.0 / math.sqrt(
        lax.axis_size("rep") * lax.axis_size("dp") * lax.axis_size("seq") * positions
    )
    grad_qkv, grad_proj = assemble(
        nums, gather_blocks(first_block, place), gather_blocks(second_block, place, small), place, factor, group
    )
    inner = swapped(after(inner, second_total), "seq", 1)
    outer = edge_partner(after(outer, second_total))
    padded_back = jnp.pad(
        with_halo(back_mixed, inner.astype(F32), outer.astype(F32), core), spatial
    )
    grad_tokens = (
        back_mixed + tap_sum(padded_back, conv_weight, depth, height, width, True)
    ).astype(BF)
    for small in steps:
        pass
    small = small * factor
    taps = conv_weight.shape[0]
    return (
        output[None],
        grad_tokens[None],
        grad_qkv,
        grad_proj,
        small[:taps],
        small[taps],
        small[taps + 1, :head_count],
    )


def solution(mesh):
    block = P(("rep", "dp"), "seq", None, None, None)
    rows = P("dp", None)
    return jax.shard_map(
        per_device,
        mesh=mesh,
        in_specs=(block, block, rows, rows, P(), P(), P(), P()),
        out_specs=(block, block, rows, rows, P(), P(), P()),
        check_vma=False,
    )
```

```python
import functools
import math

import jax
import jax.numpy as jnp
from jax import lax
from jax.experimental import pallas as pl
from jax.experimental.pallas import tpu as pltpu
from jax.sharding import PartitionSpec as P

HALF = 8
LOG2_E = math.log2(math.e)
BF = jnp.bfloat16
F32 = jnp.float32


def busy(microseconds, megabytes):
    return pl.CostEstimate(
        flops=int(microseconds * 0.5e7), bytes_accessed=int(megabytes * 0.1e6), transcendentals=0
    )


def swapped(x, axis, flip):
    count = 1
    for name in (axis,) if isinstance(axis, str) else axis:
        count = count * lax.axis_size(name)
    return lax.ppermute(x, axis, [(i, i ^ flip) for i in range(count)])


def window_partner(x):
    count = lax.axis_size("seq")
    pairs = [(i, (i + 1) % count if i % 2 else (i - 1) % count) for i in range(count)]
    return lax.ppermute(x, "seq", pairs)


def edge_partner(x):
    count = lax.axis_size("seq")
    pairs = [(i, i + 1) for i in range(1, count - 1, 2)]
    return lax.ppermute(x, "seq", pairs + [(j, i) for i, j in pairs])


def with_halo(x, inner, outer, core):
    low = core == 0
    return jnp.concatenate(
        [jnp.where(low, outer, inner)[None], x, jnp.where(low, inner, outer)[None]], axis=0
    )


def tap_sum(padded, weight, slab_depth, height, grid_width, flipped):
    summed = jnp.zeros((slab_depth, height, grid_width, padded.shape[-1]), F32)
    for a in range(3):
        for b in range(3):
            for e in range(3):
                starts = (2 - a, 2 - b, 2 - e) if flipped else (a, b, e)
                part = padded[
                    starts[0] : starts[0] + slab_depth,
                    starts[1] : starts[1] + height,
                    starts[2] : starts[2] + grid_width,
                ]
                summed = summed + weight[9 * a + 3 * b + e] * part.astype(F32)
    return summed


OVER_ROWS = (((0,), (0,)), ((), ()))
OVER_LANES = (((1,), (1,)), ((), ()))


def allowed_pairs(nums, n):
    rows_shift, cols_shift, second = nums[0], nums[1], nums[2]

    def code(dim):
        t = lax.broadcasted_iota(jnp.int32, (n, n), dim)
        first_bit = jnp.where(((t >> 3) & 7) < rows_shift, 2, 0)
        return first_bit + jnp.where((t & 7) < cols_shift, second, 0)

    return jnp.where(code(0) == code(1), 1.0, 0.0).astype(F32)


def project(nums, x, mine, got, other, group, qkv):
    channels = x.shape[1]
    half = channels // 2
    quarter = half // 2
    low_rows, low_core = nums[3] == 0, nums[4] == 0
    x = x.astype(F32)
    x_mine = jnp.where(low_rows, x[:, :half], x[:, half:])
    x_peer = jnp.where(low_rows, x[:, half:], x[:, :half])
    x_got = jnp.where(low_core, x_peer[:, :quarter], x_peer[:, quarter:]).astype(BF)
    x_other = jnp.where(low_core, x_peer[:, quarter:], x_peer[:, :quarter]).astype(BF)
    x_mine = x_mine.astype(BF)
    for part in range(3):
        total = jnp.dot(x_mine, mine(part), preferred_element_type=F32)
        total = total + jnp.dot(x_got, got(part), preferred_element_type=F32)
        total = total + jnp.dot(x_other, other(part), preferred_element_type=F32)
        qkv[part * group : (part + 1) * group, :] = total.T.astype(BF)


def attend(head_dim, allowed, scale, base, group, qkv, ba, ba_low, att, back, gs):
    def unit(raw):
        inverse = lax.rsqrt(jnp.sum(raw * raw, axis=0, keepdims=True) + 1.0)
        return inverse, (raw * inverse).astype(BF)

    def radius_back(raw, inverse, grad):
        inner = jnp.sum(raw * grad, axis=0, keepdims=True)
        return grad * inverse - raw * (inner * (inverse * inverse * inverse))

    def one_head(h):
        def rows(start):
            return pl.ds(pl.multiple_of(start + h * head_dim, head_dim), head_dim)

        s = scale[base + h]
        qf = qkv[rows(0), :].astype(F32)
        kf = qkv[rows(group), :].astype(F32)
        v = qkv[rows(2 * group), :]
        b = ba[rows(ba_low), :]
        iq, uq = unit(qf)
        ik, uk = unit(kf)
        cosine = lax.dot_general(uk, uq, OVER_ROWS, preferred_element_type=F32)
        back_prob = lax.dot_general(v, b, OVER_ROWS, preferred_element_type=F32)
        expo = jnp.exp2(cosine * (s * LOG2_E)) * allowed
        inverse = 1.0 / jnp.sum(expo, axis=0, keepdims=True)
        weights = (expo * inverse).astype(BF)
        att[rows(0), :] = jnp.dot(v, weights, preferred_element_type=F32).astype(BF)
        mean = jnp.sum(expo * back_prob, axis=0, keepdims=True) * inverse
        scaled = expo * (inverse * s) * (back_prob - mean)
        gs[pl.ds(h, 1), :] = jnp.sum(scaled * cosine, axis=0, keepdims=True) * (1.0 / s)
        scaled = scaled.astype(BF)
        buq = jnp.dot(uk, scaled, preferred_element_type=F32)
        buk = lax.dot_general(uq, scaled, OVER_LANES, preferred_element_type=F32)
        bv = lax.dot_general(b, weights, OVER_LANES, preferred_element_type=F32)
        back[rows(0), :] = radius_back(qf, iq, buq).astype(BF)
        back[rows(group), :] = radius_back(kf, ik, buk).astype(BF)
        back[rows(2 * group), :] = bv.astype(BF)

    count = group // head_dim
    unrolled = next(u for u in (10, 8, 4, 2, 1) if count % u == 0)

    def body(i, carry):
        for u in range(unrolled):
            one_head(i * unrolled + u)
        return carry

    lax.fori_loop(0, count // unrolled, body, 0)


def first_kernel(group, head_dim, nums, scale, xm, xg, cot, w_qkv, w_proj, got, other, *outs):
    send, att, ba, gs, qkv = outs
    channels = xm.shape[1]
    half = channels // 2
    x = jnp.concatenate([xm[...], xg[...]], axis=0)

    def columns(ref, base):
        return lambda part: ref[:, base + part * channels : base + part * channels + group]

    far = (columns(got, channels), columns(other, channels))
    project(nums, x, columns(w_qkv, 0), *far, group, qkv)
    quarter = half // 2
    dp, core = nums[3], nums[4]

    def back_rows(start, count, weight):
        value = lax.dot_general(weight, cot[...], OVER_LANES, preferred_element_type=F32)
        ba[pl.ds(pl.multiple_of(start, quarter), count), :] = value.astype(BF)

    back_rows(dp * half, half, w_proj[...])
    back_rows((1 - dp) * half + core * quarter, quarter, got[:, :channels])
    back_rows((1 - dp) * half + (1 - core) * quarter, quarter, other[:, :channels])
    allowed = allowed_pairs(nums, x.shape[0])
    attend(head_dim, allowed, scale, 0, group, qkv, ba, 0, att, send, gs)


def second_kernel(group, head_dim, nums, scale, xm, xg, order, ba, att_first, *refs):
    send_first, w_qkv, got, other, send, att_rows, mine, window, att_mine, gs, qkv, att = refs
    channels = xm.shape[1]
    half = channels // 2
    low = channels - group
    x = jnp.concatenate([xm[...], xg[...]], axis=0)

    def columns(ref, base):
        return lambda part: ref[:, base + part * channels : base + part * channels + group]

    far = (columns(got, channels + low), columns(other, channels + low))
    project(nums, x, columns(w_qkv, low), *far, group, qkv)
    allowed = allowed_pairs(nums, x.shape[0])
    attend(head_dim, allowed, scale, low // head_dim, group, qkv, ba, low, att, send, gs)

    def ordered(rows):
        total = jnp.dot(order[rows, :low], att_first[...], preferred_element_type=F32)
        total = total + jnp.dot(order[rows, low:], att[...], preferred_element_type=F32)
        return total.astype(BF)

    att_rows[...] = ordered(slice(0, half))
    send[3 * group :, :] = ordered(slice(half, channels))
    back_through(low, nums, send_first, send, w_qkv, got, other, att_first, att, mine, window, att_mine)


def attention_call(body, name, group, head_dim, outs, operands, megabytes, scratch=()):
    n = 2 * operands[2].shape[0]
    vmem = pl.BlockSpec(memory_space=pltpu.VMEM)
    smem = pl.BlockSpec(memory_space=pltpu.SMEM)
    shapes = tuple(jax.ShapeDtypeStruct(shape, BF) for shape in outs)
    shapes = shapes + (jax.ShapeDtypeStruct((group // head_dim, n), F32),)
    return pl.pallas_call(
        functools.partial(body, group, head_dim),
        out_shape=shapes,
        in_specs=[smem, smem] + [vmem] * (len(operands) - 2),
        out_specs=(vmem,) * len(shapes),
        scratch_shapes=[pltpu.VMEM((rows, n), BF) for rows in (3 * group, *scratch)],
        compiler_params=pltpu.CompilerParams(vmem_limit_bytes=megabytes * 1024 * 1024),
        cost_estimate=busy(5 + 0.5 * (group // head_dim), 8),
        name=name,
    )(*operands)


def stage_kernel(core, w_qkv, w_proj, tokens, weights, inner, outer, sems):
    rows, channels = weights.shape[0], w_proj.shape[1]
    mine = pl.ds(pl.multiple_of(core[0] * rows, rows), rows)
    copies = (
        (w_proj.at[mine, :], weights.at[:, :channels]),
        (w_qkv.at[mine, :], weights.at[:, channels:]),
        (tokens.at[0, core[0]], outer),
        (tokens.at[0, 1 - core[0]], inner),
    )
    started = [pltpu.make_async_copy(x, y, sems.at[i]) for i, (x, y) in enumerate(copies)]
    for copy in started:
        copy.start()
    for copy in started:
        copy.wait()


def stage(core, w_qkv, w_proj, tokens):
    channels = w_proj.shape[1]
    rows = w_proj.shape[0] // 2
    anywhere = pl.BlockSpec(memory_space=pl.ANY)
    vmem = pl.BlockSpec(memory_space=pltpu.VMEM)
    plane = jax.ShapeDtypeStruct(tokens.shape[2:], BF)
    return pl.pallas_call(
        stage_kernel,
        out_shape=(jax.ShapeDtypeStruct((rows, 4 * channels), BF), plane, plane),
        in_specs=[pl.BlockSpec(memory_space=pltpu.SMEM)] + [anywhere] * 3,
        out_specs=(vmem,) * 3,
        scratch_shapes=[pltpu.SemaphoreType.DMA((4,))],
        cost_estimate=busy(2.5, 4),
        name="stage",
    )(core[None].astype(jnp.int32), w_qkv, w_proj, tokens)


def back_through(group, nums, first, second, w_qkv, got, other, att1, att2, mine, send, att_mine):
    n = first.shape[1]
    half = n // 2
    channels = att_mine.shape[1]
    rest = channels - group
    low_rows, low_core = nums[3] == 0, nums[4] == 0

    def through(weight, base):
        total = None
        for part in range(3):
            low = base + part * channels
            for columns, rows, ref in (
                (slice(low, low + group), slice(part * group, (part + 1) * group), first),
                (slice(low + group, low + channels), slice(part * rest, (part + 1) * rest), second),
            ):
                term = jnp.dot(weight[:, columns], ref[rows, :], preferred_element_type=F32)
                total = term if total is None else total + term
        return total

    from_mine = through(w_qkv, 0)
    from_got = through(got, channels)
    from_other = through(other, channels)
    from_peer = jnp.concatenate(
        [jnp.where(low_core, from_got, from_other), jnp.where(low_core, from_other, from_got)]
    )
    shifted = jnp.concatenate(
        [jnp.where(low_rows, from_mine, from_peer), jnp.where(low_rows, from_peer, from_mine)]
    )
    shifted = shifted.T.astype(BF)
    mine[...] = shifted[:half]
    send[:half, :] = shifted[half:]
    for low, ref in ((0, att1), (group, att2)):
        wide = slice(low, low + ref.shape[0])
        turned = ref[...].astype(F32).T.astype(BF)
        att_mine[:, wide] = turned[:half]
        send[half:, wide] = turned[half:]


def after(x, *others):
    anywhere = pl.BlockSpec(memory_space=pl.ANY)

    def nothing(*refs):
        del refs

    return pl.pallas_call(
        nothing,
        out_shape=jax.ShapeDtypeStruct(x.shape, x.dtype),
        in_specs=[anywhere] * (1 + len(others)),
        out_specs=anywhere,
        input_output_aliases={0: 0},
        name="ordered",
    )(x, *others)


def pick(x, index, axis):
    return lax.dynamic_index_in_dim(x, index, axis, keepdims=False)


def tree_sum(parts):
    while len(parts) > 1:
        parts = [a + b for a, b in zip(parts[::2], parts[1::2])]
    return parts[0]


def chip_stages(chips):
    stages = []
    stride = 1
    while stride < chips:
        radix = 4 if (chips // stride) % 4 == 0 else 2
        stages.append((radix, stride))
        stride = stride * radix
    return stages


class Place:
    def __init__(self, channels):
        self.seq = lax.axis_index("seq")
        self.core = self.seq % 2
        self.rep, self.dp = lax.axis_index("rep"), lax.axis_index("dp")
        self.stages = chip_stages(lax.axis_size("seq") // 2)
        self.split = self.stages[0][0] if self.stages else 1
        self.digit = (self.seq // 2) % self.split
        self.rows = channels // (8 * self.split)
        self.channels = channels

    def row_order(self):
        p = jnp.arange(self.channels)
        inner = p % self.rows
        z = (p // self.rows) % self.split
        square = (p // (self.rows * self.split)) % 4
        pair = p // (self.rows * self.split * 4)
        rep, dp = self.rep ^ (square >> 1), self.dp ^ (square & 1)
        target = ((dp * 2 + (self.core ^ pair)) * 2 + rep) * self.split + (self.digit ^ z)
        target = target * self.rows + inner
        return (target[:, None] == jnp.arange(self.channels)[None, :]).astype(BF)


def gradient_kernel(width, has_proj, *refs):
    if has_proj:
        xm, xg, bm, bg, am, cm, cg, own, s1, s2, s3 = refs
    else:
        xm, xg, bm, bg, own, s1, s2, s3 = refs
    quarter = own.shape[0]
    tile = 384
    x_far = xg[...]

    def put(first, total):
        columns = slice(first, first + tile)
        own[:, columns] = total[:quarter]
        for k, ref in enumerate((s1, s2, s3)):
            ref[:, columns] = total[(k + 1) * quarter : (k + 2) * quarter].astype(BF)

    for first in range(0, width, tile):
        rows = slice(first, first + tile)
        total = lax.dot_general(xm[...], bm[rows, :], OVER_LANES, preferred_element_type=F32)
        put(first, total + lax.dot_general(x_far, bg[rows, :], OVER_LANES, preferred_element_type=F32))
    if has_proj:
        far = bg[width:, :]
        for first in range(0, cm.shape[1], tile):
            columns = slice(first, first + tile)
            total = jnp.dot(am[...], cm[:, columns], preferred_element_type=F32)
            put(width + first, total + jnp.dot(far, cg[:, columns], preferred_element_type=F32))


def chip_gradient(group, operands):
    rows, n = operands[0].shape
    width = 3 * group
    has_proj = len(operands) > 4
    total = width + (operands[5].shape[1] if has_proj else 0)
    vmem = pl.BlockSpec(memory_space=pltpu.VMEM)
    wire = jax.ShapeDtypeStruct((rows // 4, total), BF)
    return pl.pallas_call(
        functools.partial(gradient_kernel, width, has_proj),
        out_shape=(jax.ShapeDtypeStruct((rows // 4, total), F32), wire, wire, wire),
        in_specs=[vmem] * len(operands),
        out_specs=(vmem,) * 4,
        compiler_params=pltpu.CompilerParams(vmem_limit_bytes=12 * 1024 * 1024),
        cost_estimate=busy(1.5, 3.5),
        name="chip_gradient",
    )(*operands)


def sum_square(own, sends, place):
    got = [own] + [swapped(s, ("rep", "dp"), k + 1).astype(F32) for k, s in enumerate(sends)]
    return tree_sum(got)


def sum_chips(total, place, *others):
    parts = total.reshape(place.split, place.rows, -1)
    got = [parts[0]]
    for k in range(1, place.split):
        there = swapped(parts[k].astype(BF), "seq", 2 * k)
        got.append((after(there, *others) if others and k == 1 else there).astype(F32))
    total = tree_sum(got)
    for radix, stride in place.stages[1:]:
        held = total.astype(BF)
        got = [swapped(held, "seq", 2 * k * stride) if k else held for k in range(radix)]
        total = tree_sum([g.astype(F32) for g in got])
    return total.astype(BF)


def gather_blocks(block, place, *others):
    got = [swapped(block, "seq", 2 * k) if k else block for k in range(place.split)]
    if others:
        got[-1] = after(got[-1], *others)
    chips = jnp.concatenate(got)
    other_rep = swapped(chips, "rep", 1)
    return chips, other_rep, swapped(chips, "seq", 1), swapped(other_rep, "seq", 1)


def assemble_kernel(split, factor, group, at, *refs):
    first, second = refs[:4], refs[4:8]
    qkv, proj = refs[8], refs[9]
    rows = first[0].shape[0] // split
    third = qkv.shape[1] // 3
    rest = third - group
    for pair in range(2):
        for square in range(2):
            index = 2 * pair + square
            base = ((at[4] ^ pair) * 2 + (at[5] ^ square)) * split
            for z in range(split):
                here = slice(z * rows, (z + 1) * rows)
                there = pl.ds(pl.multiple_of((base + (at[6] ^ z)) * rows, rows), rows)
                for part in range(3):
                    low, mid = part * third, part * third + group
                    a = first[index][here, part * group : (part + 1) * group]
                    qkv[there, low:mid] = a.astype(F32) * factor
                    b = second[index][here, part * rest : (part + 1) * rest]
                    qkv[there, mid : low + third] = b.astype(F32) * factor
                proj[there, :] = second[index][here, 3 * rest :].astype(F32) * factor


def assemble(nums, first, second, place, factor, group):
    rows = 4 * first[0].shape[0]
    channels = place.channels
    vmem = pl.BlockSpec(memory_space=pltpu.VMEM)
    smem = pl.BlockSpec(memory_space=pltpu.SMEM)
    return pl.pallas_call(
        functools.partial(assemble_kernel, place.split, factor, group),
        out_shape=(
            jax.ShapeDtypeStruct((rows, 3 * channels), F32),
            jax.ShapeDtypeStruct((rows, channels), F32),
        ),
        in_specs=[smem] + [vmem] * 8,
        out_specs=(vmem, vmem),
        compiler_params=pltpu.CompilerParams(vmem_limit_bytes=16 * 1024 * 1024),
        cost_estimate=busy(3, 7),
        name="assemble",
    )(nums, *first, *second)


def sum_steps(x, place):
    half = x.shape[0] // 2
    low = place.core == 0
    x = jnp.where(low, x[:half], x[half:]) + swapped(
        jnp.where(low, x[half:], x[:half]), "seq", 1
    )
    x = x + swapped(x, "rep", 1)
    yield x
    x = x + swapped(x, "dp", 1)
    yield x
    flip = 2
    while flip < lax.axis_size("seq"):
        x = x + swapped(x, "seq", flip)
        yield x
        flip = flip * 2
    got = swapped(x, "seq", 1)
    yield jnp.concatenate([jnp.where(low, x, got), jnp.where(low, got, x)])


def rows_of_both(mine, got, other, place):
    half = got.shape[0]
    m0, m1 = mine[:half], mine[half:]
    p0 = jnp.where(place.core == 0, got, other)
    p1 = jnp.where(place.core == 0, other, got)
    low = place.dp == 0
    return jnp.concatenate(
        [jnp.where(low, a, b) for a, b in ((m0, p0), (m1, p1), (p0, m0), (p1, m1))]
    )


GROUP_HEADS = 16


def shifted_fields(before, slab, behind, lanes):
    planes = jnp.concatenate([before[:, :, lanes][None], slab[0, :, :, :, lanes], behind[:, :, lanes][None]])
    planes = planes.astype(F32)
    row = jnp.zeros_like(planes[:, :1])
    planes = jnp.concatenate([row, planes, row], axis=1)
    column = jnp.zeros_like(planes[:, :, :1])
    width = planes.shape[2]
    yield jnp.concatenate([column, planes[:, :, : width - 1]], axis=2)
    yield planes
    yield jnp.concatenate([planes[:, :, 1:], column], axis=2)


def field_forward_kernel(nums, slab, before, behind, weight, gain, mixed, mine, theirs):
    depth, height, width, channels = mixed.shape
    tile = 128
    for start in range(0, channels, tile):
        lanes = slice(start, start + tile)
        total = slab[0, :, :, :, lanes].astype(F32)
        for e, shifted in enumerate(shifted_fields(before, slab, behind, lanes)):
            for a in range(3):
                for b in range(3):
                    t = 9 * a + 3 * b + e
                    factor = weight[t : t + 1, lanes].reshape(1, 1, 1, tile)
                    total = total + factor * shifted[a : a + depth, b : b + height]
        mixed[:, :, :, lanes] = total
    rows = depth * height
    field = mixed[...].reshape(rows, width, channels)
    field = field - jnp.mean(field, axis=-1, keepdims=True)
    std = lax.rsqrt(jnp.mean(field * field, axis=-1, keepdims=True) + 1e-05)
    field = field * std * gain[...].reshape(1, 1, channels)
    low, high = field[:, :HALF], field[:, HALF:]
    column = lax.broadcasted_iota(jnp.int32, low.shape, 1)
    straight = (column >= nums[1]).astype(jnp.int32) == nums[4]
    mine[...] = jnp.where(straight, low, high).reshape(rows * HALF, channels).astype(BF)
    theirs[...] = jnp.where(straight, high, low).reshape(rows * HALF, channels).astype(BF)


def field_forward(operands):
    shape = operands[1].shape[1:]
    vmem = pl.BlockSpec(memory_space=pltpu.VMEM)
    smem = pl.BlockSpec(memory_space=pltpu.SMEM)
    half = jax.ShapeDtypeStruct((shape[0] * shape[1] * HALF, shape[3]), BF)
    return pl.pallas_call(
        field_forward_kernel,
        out_shape=(jax.ShapeDtypeStruct(shape, F32), half, half),
        in_specs=[smem] + [vmem] * (len(operands) - 1),
        out_specs=(vmem,) * 3,
        compiler_params=pltpu.CompilerParams(vmem_limit_bytes=24 * 1024 * 1024),
        cost_estimate=busy(1, 2),
        name="field_forward",
    )(*operands)


def into_field(nums, mine, theirs):
    count = mine.shape[0] // HALF
    mine = mine.astype(F32).reshape(count, HALF, -1)
    theirs = theirs.astype(F32).reshape(count, HALF, -1)
    column = lax.broadcasted_iota(jnp.int32, mine.shape, 1)
    low = (column >= nums[1]).astype(jnp.int32) == nums[4]
    return jnp.concatenate([jnp.where(low, mine, theirs), jnp.where(low, theirs, mine)], axis=1)


def field_kernel(*refs):
    nums, back, att, got, mixed, cot, slab, before, behind, gain, scale1, scale2 = refs[:12]
    w_mine, w_got, w_other = refs[12:15]
    bm, inner, outer, out, small = refs[15:]
    depth, height, width, channels = mixed.shape
    half = back.shape[0]
    rows = depth * height
    restored = into_field(nums, att[...], got[half:, :]).reshape(rows * width, channels)
    low_rows, low_core = nums[3] == 0, nums[4] == 0
    side, part = channels // 2, channels // 4
    r_mine = jnp.where(low_rows, restored[:, :side], restored[:, side:]).astype(BF)
    r_peer = jnp.where(low_rows, restored[:, side:], restored[:, :side])
    r_got = jnp.where(low_core, r_peer[:, :part], r_peer[:, part:]).astype(BF)
    r_other = jnp.where(low_core, r_peer[:, part:], r_peer[:, :part]).astype(BF)
    projected = jnp.dot(r_mine, w_mine[...], preferred_element_type=F32)
    projected = projected + jnp.dot(r_got, w_got[...], preferred_element_type=F32)
    projected = projected + jnp.dot(r_other, w_other[...], preferred_element_type=F32)
    out[...] = (mixed[...] + projected.reshape(mixed.shape)).astype(BF)

    normed = into_field(nums, back[...], got[:half, :])
    field = mixed[...].reshape(rows, width, channels)
    field = field - jnp.mean(field, axis=-1, keepdims=True)
    std = lax.rsqrt(jnp.mean(field * field, axis=-1, keepdims=True) + 1e-05)
    field = field * std
    small[27:28, :] = jnp.sum(jnp.sum(normed * field, axis=0), axis=0, keepdims=True)
    grad = normed * gain[...].reshape(1, 1, channels)
    mean = jnp.mean(grad, axis=-1, keepdims=True)
    slope = jnp.mean(grad * field, axis=-1, keepdims=True)
    value = cot[...].astype(F32).reshape(rows, width, channels) + std * (grad - mean - field * slope)
    bm[...] = value.reshape(mixed.shape)
    first, last = value[:height].astype(BF), value[rows - height :].astype(BF)
    inner[...] = jnp.where(low_core, last.astype(F32), first.astype(F32)).astype(BF)
    outer[...] = jnp.where(low_core, first.astype(F32), last.astype(F32)).astype(BF)

    tile = 128
    for start in range(0, channels, tile):
        lanes = slice(start, start + tile)
        mixed_back = bm[:, :, :, lanes]
        for e, shifted in enumerate(shifted_fields(before, slab, behind, lanes)):
            for a in range(3):
                for b in range(3):
                    product = mixed_back * shifted[a : a + depth, b : b + height]
                    row = jnp.sum(jnp.sum(product, axis=(0, 1)), axis=0, keepdims=True)
                    small[9 * a + 3 * b + e : 9 * a + 3 * b + e + 1, lanes] = row
    sums = jnp.concatenate([scale1[...], scale2[...]], axis=0)
    sums = jnp.sum(sums, axis=1, keepdims=True)
    heads = sums.shape[0]
    same = lax.broadcasted_iota(jnp.int32, (heads, channels), 0) == lax.broadcasted_iota(
        jnp.int32, (heads, channels), 1
    )
    small[28:29, :] = jnp.sum(jnp.where(same, sums, 0.0), axis=0, keepdims=True)
    small[29:32, :] = jnp.zeros((3, channels), F32)


def field_back(operands):
    mixed = operands[4]
    channels = mixed.shape[-1]
    first_columns = pl.BlockSpec((operands[-1].shape[0], channels), lambda i: (0, 0))
    vmem = pl.BlockSpec(memory_space=pltpu.VMEM)
    smem = pl.BlockSpec(memory_space=pltpu.SMEM)
    plane = jax.ShapeDtypeStruct(mixed.shape[1:], BF)
    return pl.pallas_call(
        field_kernel,
        grid=(1,),
        out_shape=(
            jax.ShapeDtypeStruct(mixed.shape, F32),
            plane,
            plane,
            jax.ShapeDtypeStruct(mixed.shape, BF),
            jax.ShapeDtypeStruct((32, mixed.shape[-1]), F32),
        ),
        in_specs=[smem] + [vmem] * (len(operands) - 3) + [first_columns] * 2,
        out_specs=(vmem,) * 5,
        compiler_params=pltpu.CompilerParams(vmem_limit_bytes=60 * 1024 * 1024),
        cost_estimate=busy(1, 2),
        name="field_back",
    )(*operands)


def per_device(tokens, cotangent, w_qkv, w_proj, conv_weight, norm_gain, head_scale, shift_offsets):
    slab = tokens[0]
    cot = cotangent[0]
    depth, height, width, channels = slab.shape
    head_count = head_scale.shape[0]
    head_dim = channels // head_count
    place = Place(channels)
    core, dp = place.core, place.dp
    rows_shift, cols_shift = shift_offsets[0], shift_offsets[1]
    positions = depth * height * width
    half = positions // 2
    columns = jnp.arange(HALF)[None, None, :, None]
    straight = (columns >= cols_shift) == (core == 1)
    group = GROUP_HEADS * head_dim

    def split_columns(field):
        low, high = field[:, :, :HALF], field[:, :, HALF:]
        return (
            jnp.where(straight, low, high).reshape(half, -1),
            jnp.where(straight, high, low).reshape(half, -1),
        )

    def join_columns(mine, theirs):
        mine = mine.reshape(depth, height, HALF, -1)
        theirs = theirs.reshape(depth, height, HALF, -1)
        return jnp.concatenate(
            [jnp.where(straight, mine, theirs), jnp.where(straight, theirs, mine)], axis=2
        )

    spatial = ((0, 0), (1, 1), (1, 1), (0, 0))
    weights_part, inner, outer = stage(core, w_qkv, w_proj, tokens)
    outer = edge_partner(outer)
    inner = swapped(inner, "seq", 1)
    weights_got = swapped(weights_part, "dp", 1)
    cot_mine, cot_theirs = split_columns(cot)
    cot_got = window_partner(cot_theirs)
    outer = after(outer, cot_got)
    before, behind = jnp.where(core == 0, outer, inner), jnp.where(core == 0, inner, outer)
    cot_window = jnp.concatenate([cot_mine, cot_got])
    order = after(place.row_order(), cot_got)

    nums = jnp.stack(
        [rows_shift, cols_shift, 1 - core, dp, core, place.rep, place.digit]
    ).astype(jnp.int32)
    mixed_field, x_mine, x_theirs = field_forward(
        (nums, tokens, before, behind, conv_weight, norm_gain)
    )
    x_theirs = window_partner(x_theirs)
    x_rows = jnp.einsum(
        "pc,tc->pt",
        order,
        jnp.concatenate([x_mine, x_theirs]),
        preferred_element_type=F32,
    ).astype(BF)
    x_other = swapped(x_rows[channels // 2 :], "seq", 1)
    x_rows = x_rows[: channels // 2]
    weights_got = after(weights_got, x_other)
    weights_other = swapped(weights_got, "seq", 1)
    cot_other = swapped(cot_window, "seq", 1)
    half_rows = channels // 2
    n = 2 * half
    send_first, att_first, back_attended, scale_first = attention_call(
        first_kernel,
        "first_heads",
        group,
        head_dim,
        ((3 * group, n), (group, n), (channels, n)),
        (nums, head_scale, x_mine, x_theirs, cot_window, w_qkv, w_proj, weights_got, weights_other),
        24,
    )
    got_first = swapped(send_first, "seq", 1)
    own, *sends = chip_gradient(group, (x_rows, x_other, send_first, got_first))
    rest = channels - group
    send_second, att_rows, back_mine, window_send, att_mine, scale_second = attention_call(
        second_kernel,
        "second_heads",
        rest,
        head_dim,
        (
            (3 * rest + half_rows, n),
            (half_rows, n),
            (half, channels),
            (n, channels),
            (half, channels),
        ),
        (
            nums,
            head_scale,
            x_mine,
            x_theirs,
            order,
            after(back_attended, own),
            att_first,
            send_first,
            w_qkv,
            weights_got,
            weights_other,
        ),
        60,
        (rest,),
    )
    first_own, first_sends = own, sends
    got_second = swapped(send_second, "seq", 1)
    first_total = sum_square(first_own, first_sends, place)
    own, *sends = chip_gradient(
        rest,
        (
            after(x_rows, back_mine, first_total),
            x_other,
            send_second,
            got_second,
            att_rows,
            cot_window,
            cot_other,
        )
    )
    window_got = after(window_partner(window_send), own)
    back_mixed, inner, outer, output, small = field_back(
        (
            nums,
            back_mine,
            att_mine,
            window_got,
            mixed_field,
            cot,
            tokens,
            before,
            behind,
            norm_gain,
            scale_first,
            scale_second,
            w_proj,
            weights_got,
            weights_other,
        )
    )
    second_total = sum_square(after(own, small), sends, place)
    first_block = sum_chips(first_total, place, second_total)
    steps = sum_steps(after(small, second_total), place)
    small = next(steps)
    small = next(steps)
    second_block = sum_chips(second_total, place)
    small = next(steps)
    factor = 1.0 / math.sqrt(
        lax.axis_size("rep") * lax.axis_size("dp") * lax.axis_size("seq") * positions
    )
    grad_qkv, grad_proj = assemble(
        nums, gather_blocks(first_block, place), gather_blocks(second_block, place, small), place, factor, group
    )
    inner = swapped(after(inner, second_total), "seq", 1)
    outer = edge_partner(after(outer, second_total))
    padded_back = jnp.pad(
        with_halo(back_mixed, inner.astype(F32), outer.astype(F32), core), spatial
    )
    grad_tokens = (
        back_mixed + tap_sum(padded_back, conv_weight, depth, height, width, True)
    ).astype(BF)
    for small in steps:
        pass
    small = small * factor
    taps = conv_weight.shape[0]
    return (
        output[None],
        grad_tokens[None],
        grad_qkv,
        grad_proj,
        small[:taps],
        small[taps],
        small[taps + 1, :head_count],
    )


def solution(mesh):
    block = P(("rep", "dp"), "seq", None, None, None)
    rows = P("dp", None)
    return jax.shard_map(
        per_device,
        mesh=mesh,
        in_specs=(block, block, rows, rows, P(), P(), P(), P()),
        out_specs=(block, block, rows, rows, P(), P(), P()),
        check_vma=False,
    )
```

```python
import functools
import math

import jax
import jax.numpy as jnp
from jax import lax
from jax.experimental import pallas as pl
from jax.experimental.pallas import tpu as pltpu
from jax.sharding import PartitionSpec as P

HALF = 8
LOG2_E = math.log2(math.e)
BF = jnp.bfloat16
F32 = jnp.float32


def busy(microseconds, megabytes):
    return pl.CostEstimate(
        flops=int(microseconds * 0.5e7), bytes_accessed=int(megabytes * 0.1e6), transcendentals=0
    )


def swapped(x, axis, flip):
    count = 1
    for name in (axis,) if isinstance(axis, str) else axis:
        count = count * lax.axis_size(name)
    return lax.ppermute(x, axis, [(i, i ^ flip) for i in range(count)])


def window_partner(x):
    count = lax.axis_size("seq")
    pairs = [(i, (i + 1) % count if i % 2 else (i - 1) % count) for i in range(count)]
    return lax.ppermute(x, "seq", pairs)


def edge_partner(x):
    count = lax.axis_size("seq")
    pairs = [(i, i + 1) for i in range(1, count - 1, 2)]
    return lax.ppermute(x, "seq", pairs + [(j, i) for i, j in pairs])


def with_halo(x, inner, outer, core):
    low = core == 0
    return jnp.concatenate(
        [jnp.where(low, outer, inner)[None], x, jnp.where(low, inner, outer)[None]], axis=0
    )


def tap_sum(padded, weight, slab_depth, height, grid_width, flipped):
    summed = jnp.zeros((slab_depth, height, grid_width, padded.shape[-1]), F32)
    for a in range(3):
        for b in range(3):
            for e in range(3):
                starts = (2 - a, 2 - b, 2 - e) if flipped else (a, b, e)
                part = padded[
                    starts[0] : starts[0] + slab_depth,
                    starts[1] : starts[1] + height,
                    starts[2] : starts[2] + grid_width,
                ]
                summed = summed + weight[9 * a + 3 * b + e] * part.astype(F32)
    return summed


OVER_ROWS = (((0,), (0,)), ((), ()))
OVER_LANES = (((1,), (1,)), ((), ()))


def allowed_pairs(nums, n):
    rows_shift, cols_shift, second = nums[0], nums[1], nums[2]

    def code(dim):
        t = lax.broadcasted_iota(jnp.int32, (n, n), dim)
        first_bit = jnp.where(((t >> 3) & 7) < rows_shift, 2, 0)
        return first_bit + jnp.where((t & 7) < cols_shift, second, 0)

    return jnp.where(code(0) == code(1), 1.0, 0.0).astype(F32)


def project(nums, x, mine, got, other, group, qkv):
    channels = x.shape[1]
    half = channels // 2
    quarter = half // 2
    low_rows, low_core = nums[3] == 0, nums[4] == 0
    x = x.astype(F32)
    x_mine = jnp.where(low_rows, x[:, :half], x[:, half:])
    x_peer = jnp.where(low_rows, x[:, half:], x[:, :half])
    x_got = jnp.where(low_core, x_peer[:, :quarter], x_peer[:, quarter:]).astype(BF)
    x_other = jnp.where(low_core, x_peer[:, quarter:], x_peer[:, :quarter]).astype(BF)
    x_mine = x_mine.astype(BF)
    for part in range(3):
        total = jnp.dot(x_mine, mine(part), preferred_element_type=F32)
        total = total + jnp.dot(x_got, got(part), preferred_element_type=F32)
        total = total + jnp.dot(x_other, other(part), preferred_element_type=F32)
        qkv[part * group : (part + 1) * group, :] = total.T.astype(BF)


def attend(head_dim, allowed, scale, base, group, qkv, ba, ba_low, att, back, gs):
    def unit(raw):
        inverse = lax.rsqrt(jnp.sum(raw * raw, axis=0, keepdims=True) + 1.0)
        return inverse, (raw * inverse).astype(BF)

    def radius_back(raw, inverse, grad):
        inner = jnp.sum(raw * grad, axis=0, keepdims=True)
        return grad * inverse - raw * (inner * (inverse * inverse * inverse))

    def one_head(h):
        def rows(start):
            return pl.ds(pl.multiple_of(start + h * head_dim, head_dim), head_dim)

        s = scale[base + h]
        qf = qkv[rows(0), :].astype(F32)
        kf = qkv[rows(group), :].astype(F32)
        v = qkv[rows(2 * group), :]
        b = ba[rows(ba_low), :]
        iq, uq = unit(qf)
        ik, uk = unit(kf)
        cosine = lax.dot_general(uk, uq, OVER_ROWS, preferred_element_type=F32)
        back_prob = lax.dot_general(v, b, OVER_ROWS, preferred_element_type=F32)
        expo = jnp.exp2(cosine * (s * LOG2_E)) * allowed
        inverse = 1.0 / jnp.sum(expo, axis=0, keepdims=True)
        weights = (expo * inverse).astype(BF)
        att[rows(0), :] = jnp.dot(v, weights, preferred_element_type=F32).astype(BF)
        mean = jnp.sum(expo * back_prob, axis=0, keepdims=True) * inverse
        scaled = expo * (inverse * s) * (back_prob - mean)
        gs[pl.ds(h, 1), :] = jnp.sum(scaled * cosine, axis=0, keepdims=True) * (1.0 / s)
        scaled = scaled.astype(BF)
        buq = jnp.dot(uk, scaled, preferred_element_type=F32)
        buk = lax.dot_general(uq, scaled, OVER_LANES, preferred_element_type=F32)
        bv = lax.dot_general(b, weights, OVER_LANES, preferred_element_type=F32)
        back[rows(0), :] = radius_back(qf, iq, buq).astype(BF)
        back[rows(group), :] = radius_back(kf, ik, buk).astype(BF)
        back[rows(2 * group), :] = bv.astype(BF)

    count = group // head_dim
    unrolled = next(u for u in (10, 8, 4, 2, 1) if count % u == 0)

    def body(i, carry):
        for u in range(unrolled):
            one_head(i * unrolled + u)
        return carry

    lax.fori_loop(0, count // unrolled, body, 0)


def first_kernel(group, head_dim, nums, scale, xm, xg, cot, w_qkv, w_proj, got, other, *outs):
    send, att, ba, gs, qkv = outs
    channels = xm.shape[1]
    half = channels // 2
    x = jnp.concatenate([xm[...], xg[...]], axis=0)

    def columns(ref, base):
        return lambda part: ref[:, base + part * channels : base + part * channels + group]

    far = (columns(got, channels), columns(other, channels))
    project(nums, x, columns(w_qkv, 0), *far, group, qkv)
    quarter = half // 2
    dp, core = nums[3], nums[4]

    def back_rows(start, count, weight):
        value = lax.dot_general(weight, cot[...], OVER_LANES, preferred_element_type=F32)
        ba[pl.ds(pl.multiple_of(start, quarter), count), :] = value.astype(BF)

    back_rows(dp * half, half, w_proj[...])
    back_rows((1 - dp) * half + core * quarter, quarter, got[:, :channels])
    back_rows((1 - dp) * half + (1 - core) * quarter, quarter, other[:, :channels])
    allowed = allowed_pairs(nums, x.shape[0])
    attend(head_dim, allowed, scale, 0, group, qkv, ba, 0, att, send, gs)


def second_kernel(group, head_dim, nums, scale, xm, xg, order, ba, att_first, *refs):
    send_first, w_qkv, got, other, send, att_rows, mine, window, att_mine, gs, qkv, att = refs
    channels = xm.shape[1]
    half = channels // 2
    low = channels - group
    x = jnp.concatenate([xm[...], xg[...]], axis=0)

    def columns(ref, base):
        return lambda part: ref[:, base + part * channels : base + part * channels + group]

    far = (columns(got, channels + low), columns(other, channels + low))
    project(nums, x, columns(w_qkv, low), *far, group, qkv)
    allowed = allowed_pairs(nums, x.shape[0])
    attend(head_dim, allowed, scale, low // head_dim, group, qkv, ba, low, att, send, gs)

    def ordered(rows):
        total = jnp.dot(order[rows, :low], att_first[...], preferred_element_type=F32)
        total = total + jnp.dot(order[rows, low:], att[...], preferred_element_type=F32)
        return total.astype(BF)

    att_rows[...] = ordered(slice(0, half))
    send[3 * group :, :] = ordered(slice(half, channels))
    back_through(low, nums, send_first, send, w_qkv, got, other, att_first, att, mine, window, att_mine)


def attention_call(body, name, group, head_dim, outs, operands, megabytes, scratch=()):
    n = 2 * operands[2].shape[0]
    vmem = pl.BlockSpec(memory_space=pltpu.VMEM)
    smem = pl.BlockSpec(memory_space=pltpu.SMEM)
    shapes = tuple(jax.ShapeDtypeStruct(shape, BF) for shape in outs)
    shapes = shapes + (jax.ShapeDtypeStruct((group // head_dim, n), F32),)
    return pl.pallas_call(
        functools.partial(body, group, head_dim),
        out_shape=shapes,
        in_specs=[smem, smem] + [vmem] * (len(operands) - 2),
        out_specs=(vmem,) * len(shapes),
        scratch_shapes=[pltpu.VMEM((rows, n), BF) for rows in (3 * group, *scratch)],
        compiler_params=pltpu.CompilerParams(vmem_limit_bytes=megabytes * 1024 * 1024),
        cost_estimate=busy(5 + 0.5 * (group // head_dim), 8),
        name=name,
    )(*operands)


def stage_kernel(core, w_qkv, w_proj, tokens, weights, inner, outer, sems):
    rows, channels = weights.shape[0], w_proj.shape[1]
    mine = pl.ds(pl.multiple_of(core[0] * rows, rows), rows)
    copies = (
        (w_proj.at[mine, :], weights.at[:, :channels]),
        (w_qkv.at[mine, :], weights.at[:, channels:]),
        (tokens.at[0, core[0]], outer),
        (tokens.at[0, 1 - core[0]], inner),
    )
    started = [pltpu.make_async_copy(x, y, sems.at[i]) for i, (x, y) in enumerate(copies)]
    for copy in started:
        copy.start()
    for copy in started:
        copy.wait()


def stage(core, w_qkv, w_proj, tokens):
    channels = w_proj.shape[1]
    rows = w_proj.shape[0] // 2
    anywhere = pl.BlockSpec(memory_space=pl.ANY)
    vmem = pl.BlockSpec(memory_space=pltpu.VMEM)
    plane = jax.ShapeDtypeStruct(tokens.shape[2:], BF)
    return pl.pallas_call(
        stage_kernel,
        out_shape=(jax.ShapeDtypeStruct((rows, 4 * channels), BF), plane, plane),
        in_specs=[pl.BlockSpec(memory_space=pltpu.SMEM)] + [anywhere] * 3,
        out_specs=(vmem,) * 3,
        scratch_shapes=[pltpu.SemaphoreType.DMA((4,))],
        cost_estimate=busy(2.5, 4),
        name="stage",
    )(core[None].astype(jnp.int32), w_qkv, w_proj, tokens)


def back_through(group, nums, first, second, w_qkv, got, other, att1, att2, mine, send, att_mine):
    n = first.shape[1]
    half = n // 2
    channels = att_mine.shape[1]
    rest = channels - group
    low_rows, low_core = nums[3] == 0, nums[4] == 0

    def through(weight, base):
        total = None
        for part in range(3):
            low = base + part * channels
            for columns, rows, ref in (
                (slice(low, low + group), slice(part * group, (part + 1) * group), first),
                (slice(low + group, low + channels), slice(part * rest, (part + 1) * rest), second),
            ):
                term = jnp.dot(weight[:, columns], ref[rows, :], preferred_element_type=F32)
                total = term if total is None else total + term
        return total

    from_mine = through(w_qkv, 0)
    from_got = through(got, channels)
    from_other = through(other, channels)
    from_peer = jnp.concatenate(
        [jnp.where(low_core, from_got, from_other), jnp.where(low_core, from_other, from_got)]
    )
    shifted = jnp.concatenate(
        [jnp.where(low_rows, from_mine, from_peer), jnp.where(low_rows, from_peer, from_mine)]
    )
    shifted = shifted.T.astype(BF)
    mine[...] = shifted[:half]
    send[:half, :] = shifted[half:]
    for low, ref in ((0, att1), (group, att2)):
        wide = slice(low, low + ref.shape[0])
        turned = ref[...].astype(F32).T.astype(BF)
        att_mine[:, wide] = turned[:half]
        send[half:, wide] = turned[half:]


def after(x, *others):
    anywhere = pl.BlockSpec(memory_space=pl.ANY)

    def nothing(*refs):
        del refs

    return pl.pallas_call(
        nothing,
        out_shape=jax.ShapeDtypeStruct(x.shape, x.dtype),
        in_specs=[anywhere] * (1 + len(others)),
        out_specs=anywhere,
        input_output_aliases={0: 0},
        name="ordered",
    )(x, *others)


def pick(x, index, axis):
    return lax.dynamic_index_in_dim(x, index, axis, keepdims=False)


def tree_sum(parts):
    while len(parts) > 1:
        parts = [a + b for a, b in zip(parts[::2], parts[1::2])]
    return parts[0]


def chip_stages(chips):
    stages = []
    stride = 1
    while stride < chips:
        radix = 4 if (chips // stride) % 4 == 0 else 2
        stages.append((radix, stride))
        stride = stride * radix
    return stages


class Place:
    def __init__(self, channels):
        self.seq = lax.axis_index("seq")
        self.core = self.seq % 2
        self.rep, self.dp = lax.axis_index("rep"), lax.axis_index("dp")
        self.stages = chip_stages(lax.axis_size("seq") // 2)
        self.split = self.stages[0][0] if self.stages else 1
        self.digit = (self.seq // 2) % self.split
        self.rows = channels // (8 * self.split)
        self.channels = channels

    def row_order(self):
        p = jnp.arange(self.channels)
        inner = p % self.rows
        z = (p // self.rows) % self.split
        square = (p // (self.rows * self.split)) % 4
        pair = p // (self.rows * self.split * 4)
        rep, dp = self.rep ^ (square >> 1), self.dp ^ (square & 1)
        target = ((dp * 2 + (self.core ^ pair)) * 2 + rep) * self.split + (self.digit ^ z)
        target = target * self.rows + inner
        return (target[:, None] == jnp.arange(self.channels)[None, :]).astype(BF)


def gradient_kernel(width, has_proj, *refs):
    if has_proj:
        xm, xg, bm, bg, am, cm, cg, own, s1, s2, s3 = refs
    else:
        xm, xg, bm, bg, own, s1, s2, s3 = refs
    quarter = own.shape[0]
    tile = 384
    x_far = xg[...]

    def put(first, total):
        columns = slice(first, first + tile)
        own[:, columns] = total[:quarter]
        for k, ref in enumerate((s1, s2, s3)):
            ref[:, columns] = total[(k + 1) * quarter : (k + 2) * quarter].astype(BF)

    for first in range(0, width, tile):
        rows = slice(first, first + tile)
        total = lax.dot_general(xm[...], bm[rows, :], OVER_LANES, preferred_element_type=F32)
        put(first, total + lax.dot_general(x_far, bg[rows, :], OVER_LANES, preferred_element_type=F32))
    if has_proj:
        far = bg[width:, :]
        for first in range(0, cm.shape[1], tile):
            columns = slice(first, first + tile)
            total = jnp.dot(am[...], cm[:, columns], preferred_element_type=F32)
            put(width + first, total + jnp.dot(far, cg[:, columns], preferred_element_type=F32))


def chip_gradient(group, operands):
    rows, n = operands[0].shape
    width = 3 * group
    has_proj = len(operands) > 4
    total = width + (operands[5].shape[1] if has_proj else 0)
    vmem = pl.BlockSpec(memory_space=pltpu.VMEM)
    wire = jax.ShapeDtypeStruct((rows // 4, total), BF)
    return pl.pallas_call(
        functools.partial(gradient_kernel, width, has_proj),
        out_shape=(jax.ShapeDtypeStruct((rows // 4, total), F32), wire, wire, wire),
        in_specs=[vmem] * len(operands),
        out_specs=(vmem,) * 4,
        compiler_params=pltpu.CompilerParams(vmem_limit_bytes=12 * 1024 * 1024),
        cost_estimate=busy(1.5, 3.5),
        name="chip_gradient",
    )(*operands)


def sum_square(own, sends, place):
    got = [own] + [swapped(s, ("rep", "dp"), k + 1).astype(F32) for k, s in enumerate(sends)]
    return tree_sum(got)


def sum_chips(total, place, *others):
    parts = total.reshape(place.split, place.rows, -1)
    got = [parts[0]]
    for k in range(1, place.split):
        there = swapped(parts[k].astype(BF), "seq", 2 * k)
        got.append((after(there, *others) if others and k == 1 else there).astype(F32))
    total = tree_sum(got)
    for radix, stride in place.stages[1:]:
        held = total.astype(BF)
        got = [swapped(held, "seq", 2 * k * stride) if k else held for k in range(radix)]
        total = tree_sum([g.astype(F32) for g in got])
    return total.astype(BF)


def gather_blocks(block, place, *others):
    got = [swapped(block, "seq", 2 * k) if k else block for k in range(place.split)]
    if others:
        got[-1] = after(got[-1], *others)
    chips = jnp.concatenate(got)
    other_rep = swapped(chips, "rep", 1)
    return chips, other_rep, swapped(chips, "seq", 1), swapped(other_rep, "seq", 1)


def assemble_kernel(split, factor, group, at, *refs):
    first, second = refs[:4], refs[4:8]
    qkv, proj = refs[8], refs[9]
    rows = first[0].shape[0] // split
    third = qkv.shape[1] // 3
    rest = third - group
    for pair in range(2):
        for square in range(2):
            index = 2 * pair + square
            base = ((at[4] ^ pair) * 2 + (at[5] ^ square)) * split
            for z in range(split):
                here = slice(z * rows, (z + 1) * rows)
                there = pl.ds(pl.multiple_of((base + (at[6] ^ z)) * rows, rows), rows)
                for part in range(3):
                    low, mid = part * third, part * third + group
                    a = first[index][here, part * group : (part + 1) * group]
                    qkv[there, low:mid] = a.astype(F32) * factor
                    b = second[index][here, part * rest : (part + 1) * rest]
                    qkv[there, mid : low + third] = b.astype(F32) * factor
                proj[there, :] = second[index][here, 3 * rest :].astype(F32) * factor


def assemble(nums, first, second, place, factor, group):
    rows = 4 * first[0].shape[0]
    channels = place.channels
    vmem = pl.BlockSpec(memory_space=pltpu.VMEM)
    smem = pl.BlockSpec(memory_space=pltpu.SMEM)
    return pl.pallas_call(
        functools.partial(assemble_kernel, place.split, factor, group),
        out_shape=(
            jax.ShapeDtypeStruct((rows, 3 * channels), F32),
            jax.ShapeDtypeStruct((rows, channels), F32),
        ),
        in_specs=[smem] + [vmem] * 8,
        out_specs=(vmem, vmem),
        compiler_params=pltpu.CompilerParams(vmem_limit_bytes=16 * 1024 * 1024),
        cost_estimate=busy(3, 7),
        name="assemble",
    )(nums, *first, *second)


def sum_steps(x, place, hold):
    half = x.shape[0] // 2
    low = place.core == 0
    x = jnp.where(low, x[:half], x[half:]) + swapped(
        jnp.where(low, x[half:], x[:half]), "seq", 1
    )
    x = x + swapped(x, "rep", 1)
    yield x
    x = x + swapped(x, "dp", 1)
    yield x
    flip = 2
    while flip < lax.axis_size("seq"):
        if hold:
            x = after(x, *hold)
        x = x + swapped(x, "seq", flip)
        yield x
        flip = flip * 2
    got = swapped(x, "seq", 1)
    yield jnp.concatenate([jnp.where(low, x, got), jnp.where(low, got, x)])


def rows_of_both(mine, got, other, place):
    half = got.shape[0]
    m0, m1 = mine[:half], mine[half:]
    p0 = jnp.where(place.core == 0, got, other)
    p1 = jnp.where(place.core == 0, other, got)
    low = place.dp == 0
    return jnp.concatenate(
        [jnp.where(low, a, b) for a, b in ((m0, p0), (m1, p1), (p0, m0), (p1, m1))]
    )


GROUP_HEADS = 16


def shifted_fields(before, slab, behind, lanes):
    middle = slab[0, :, :, :, lanes] if len(slab.shape) == 5 else slab[:, :, :, lanes]
    planes = [before[:, :, lanes][None], middle, behind[:, :, lanes][None]]
    planes = jnp.concatenate([p.astype(F32) for p in planes])
    row = jnp.zeros_like(planes[:, :1])
    planes = jnp.concatenate([row, planes, row], axis=1)
    column = jnp.zeros_like(planes[:, :, :1])
    width = planes.shape[2]
    yield jnp.concatenate([column, planes[:, :, : width - 1]], axis=2)
    yield planes
    yield jnp.concatenate([planes[:, :, 1:], column], axis=2)


def field_forward_kernel(nums, slab, before, behind, weight, gain, mixed, mine, theirs):
    depth, height, width, channels = mixed.shape
    tile = 128
    for start in range(0, channels, tile):
        lanes = slice(start, start + tile)
        total = slab[0, :, :, :, lanes].astype(F32)
        for e, shifted in enumerate(shifted_fields(before, slab, behind, lanes)):
            for a in range(3):
                for b in range(3):
                    t = 9 * a + 3 * b + e
                    factor = weight[t : t + 1, lanes].reshape(1, 1, 1, tile)
                    total = total + factor * shifted[a : a + depth, b : b + height]
        mixed[:, :, :, lanes] = total
    rows = depth * height
    field = mixed[...].reshape(rows, width, channels)
    field = field - jnp.mean(field, axis=-1, keepdims=True)
    std = lax.rsqrt(jnp.mean(field * field, axis=-1, keepdims=True) + 1e-05)
    field = field * std * gain[...].reshape(1, 1, channels)
    low, high = field[:, :HALF], field[:, HALF:]
    column = lax.broadcasted_iota(jnp.int32, low.shape, 1)
    straight = (column >= nums[1]).astype(jnp.int32) == nums[4]
    mine[...] = jnp.where(straight, low, high).reshape(rows * HALF, channels).astype(BF)
    theirs[...] = jnp.where(straight, high, low).reshape(rows * HALF, channels).astype(BF)


def field_forward(operands):
    shape = operands[1].shape[1:]
    vmem = pl.BlockSpec(memory_space=pltpu.VMEM)
    smem = pl.BlockSpec(memory_space=pltpu.SMEM)
    half = jax.ShapeDtypeStruct((shape[0] * shape[1] * HALF, shape[3]), BF)
    return pl.pallas_call(
        field_forward_kernel,
        out_shape=(jax.ShapeDtypeStruct(shape, F32), half, half),
        in_specs=[smem] + [vmem] * (len(operands) - 1),
        out_specs=(vmem,) * 3,
        compiler_params=pltpu.CompilerParams(vmem_limit_bytes=24 * 1024 * 1024),
        cost_estimate=busy(1, 2),
        name="field_forward",
    )(*operands)


def field_gradient_kernel(field, before, behind, weight, out):
    depth, height, width, channels = field.shape
    tile = 128
    for start in range(0, channels, tile):
        lanes = slice(start, start + tile)
        total = field[:, :, :, lanes]
        for e, shifted in enumerate(shifted_fields(before, field, behind, lanes)):
            for a in range(3):
                for b in range(3):
                    t = 9 * (2 - a) + 3 * (2 - b) + 2 - e
                    factor = weight[t : t + 1, lanes].reshape(1, 1, 1, tile)
                    total = total + factor * shifted[a : a + depth, b : b + height]
        out[:, :, :, lanes] = total.astype(BF)


def field_gradient(operands):
    vmem = pl.BlockSpec(memory_space=pltpu.VMEM)
    return pl.pallas_call(
        field_gradient_kernel,
        out_shape=jax.ShapeDtypeStruct(operands[0].shape, BF),
        in_specs=[vmem] * len(operands),
        out_specs=vmem,
        compiler_params=pltpu.CompilerParams(vmem_limit_bytes=24 * 1024 * 1024),
        cost_estimate=busy(1, 2),
        name="field_gradient",
    )(*operands)


def into_field(nums, mine, theirs):
    count = mine.shape[0] // HALF
    mine = mine.astype(F32).reshape(count, HALF, -1)
    theirs = theirs.astype(F32).reshape(count, HALF, -1)
    column = lax.broadcasted_iota(jnp.int32, mine.shape, 1)
    low = (column >= nums[1]).astype(jnp.int32) == nums[4]
    return jnp.concatenate([jnp.where(low, mine, theirs), jnp.where(low, theirs, mine)], axis=1)


def field_kernel(*refs):
    nums, back, att, got, mixed, cot, slab, before, behind, gain, scale1, scale2 = refs[:12]
    w_mine, w_got, w_other = refs[12:15]
    bm, inner, outer, out, small = refs[15:]
    depth, height, width, channels = mixed.shape
    half = back.shape[0]
    rows = depth * height
    restored = into_field(nums, att[...], got[half:, :]).reshape(rows * width, channels)
    low_rows, low_core = nums[3] == 0, nums[4] == 0
    side, part = channels // 2, channels // 4
    r_mine = jnp.where(low_rows, restored[:, :side], restored[:, side:]).astype(BF)
    r_peer = jnp.where(low_rows, restored[:, side:], restored[:, :side])
    r_got = jnp.where(low_core, r_peer[:, :part], r_peer[:, part:]).astype(BF)
    r_other = jnp.where(low_core, r_peer[:, part:], r_peer[:, :part]).astype(BF)
    projected = jnp.dot(r_mine, w_mine[...], preferred_element_type=F32)
    projected = projected + jnp.dot(r_got, w_got[...], preferred_element_type=F32)
    projected = projected + jnp.dot(r_other, w_other[...], preferred_element_type=F32)
    out[...] = (mixed[...] + projected.reshape(mixed.shape)).astype(BF)

    normed = into_field(nums, back[...], got[:half, :])
    field = mixed[...].reshape(rows, width, channels)
    field = field - jnp.mean(field, axis=-1, keepdims=True)
    std = lax.rsqrt(jnp.mean(field * field, axis=-1, keepdims=True) + 1e-05)
    field = field * std
    small[27:28, :] = jnp.sum(jnp.sum(normed * field, axis=0), axis=0, keepdims=True)
    grad = normed * gain[...].reshape(1, 1, channels)
    mean = jnp.mean(grad, axis=-1, keepdims=True)
    slope = jnp.mean(grad * field, axis=-1, keepdims=True)
    value = cot[...].astype(F32).reshape(rows, width, channels) + std * (grad - mean - field * slope)
    bm[...] = value.reshape(mixed.shape)
    first, last = value[:height].astype(BF), value[rows - height :].astype(BF)
    inner[...] = jnp.where(low_core, last.astype(F32), first.astype(F32)).astype(BF)
    outer[...] = jnp.where(low_core, first.astype(F32), last.astype(F32)).astype(BF)

    tile = 128
    for start in range(0, channels, tile):
        lanes = slice(start, start + tile)
        mixed_back = bm[:, :, :, lanes]
        for e, shifted in enumerate(shifted_fields(before, slab, behind, lanes)):
            for a in range(3):
                for b in range(3):
                    product = mixed_back * shifted[a : a + depth, b : b + height]
                    row = jnp.sum(jnp.sum(product, axis=(0, 1)), axis=0, keepdims=True)
                    small[9 * a + 3 * b + e : 9 * a + 3 * b + e + 1, lanes] = row
    sums = jnp.concatenate([scale1[...], scale2[...]], axis=0)
    sums = jnp.sum(sums, axis=1, keepdims=True)
    heads = sums.shape[0]
    same = lax.broadcasted_iota(jnp.int32, (heads, channels), 0) == lax.broadcasted_iota(
        jnp.int32, (heads, channels), 1
    )
    small[28:29, :] = jnp.sum(jnp.where(same, sums, 0.0), axis=0, keepdims=True)
    small[29:32, :] = jnp.zeros((3, channels), F32)


def field_back(operands):
    mixed = operands[4]
    channels = mixed.shape[-1]
    first_columns = pl.BlockSpec((operands[-1].shape[0], channels), lambda i: (0, 0))
    vmem = pl.BlockSpec(memory_space=pltpu.VMEM)
    smem = pl.BlockSpec(memory_space=pltpu.SMEM)
    plane = jax.ShapeDtypeStruct(mixed.shape[1:], BF)
    return pl.pallas_call(
        field_kernel,
        grid=(1,),
        out_shape=(
            jax.ShapeDtypeStruct(mixed.shape, F32),
            plane,
            plane,
            jax.ShapeDtypeStruct(mixed.shape, BF),
            jax.ShapeDtypeStruct((32, mixed.shape[-1]), F32),
        ),
        in_specs=[smem] + [vmem] * (len(operands) - 3) + [first_columns] * 2,
        out_specs=(vmem,) * 5,
        compiler_params=pltpu.CompilerParams(vmem_limit_bytes=60 * 1024 * 1024),
        cost_estimate=busy(1, 2),
        name="field_back",
    )(*operands)


def per_device(tokens, cotangent, w_qkv, w_proj, conv_weight, norm_gain, head_scale, shift_offsets):
    slab = tokens[0]
    cot = cotangent[0]
    depth, height, width, channels = slab.shape
    head_count = head_scale.shape[0]
    head_dim = channels // head_count
    place = Place(channels)
    core, dp = place.core, place.dp
    rows_shift, cols_shift = shift_offsets[0], shift_offsets[1]
    positions = depth * height * width
    half = positions // 2
    columns = jnp.arange(HALF)[None, None, :, None]
    straight = (columns >= cols_shift) == (core == 1)
    group = GROUP_HEADS * head_dim

    def split_columns(field):
        low, high = field[:, :, :HALF], field[:, :, HALF:]
        return (
            jnp.where(straight, low, high).reshape(half, -1),
            jnp.where(straight, high, low).reshape(half, -1),
        )

    def join_columns(mine, theirs):
        mine = mine.reshape(depth, height, HALF, -1)
        theirs = theirs.reshape(depth, height, HALF, -1)
        return jnp.concatenate(
            [jnp.where(straight, mine, theirs), jnp.where(straight, theirs, mine)], axis=2
        )

    spatial = ((0, 0), (1, 1), (1, 1), (0, 0))
    weights_part, inner, outer = stage(core, w_qkv, w_proj, tokens)
    outer = edge_partner(outer)
    inner = swapped(inner, "seq", 1)
    weights_got = swapped(weights_part, "dp", 1)
    cot_mine, cot_theirs = split_columns(cot)
    cot_got = window_partner(cot_theirs)
    outer = after(outer, cot_got)
    before, behind = jnp.where(core == 0, outer, inner), jnp.where(core == 0, inner, outer)
    cot_window = jnp.concatenate([cot_mine, cot_got])
    order = after(place.row_order(), cot_got)

    nums = jnp.stack(
        [rows_shift, cols_shift, 1 - core, dp, core, place.rep, place.digit]
    ).astype(jnp.int32)
    mixed_field, x_mine, x_theirs = field_forward(
        (nums, tokens, before, behind, conv_weight, norm_gain)
    )
    x_theirs = window_partner(x_theirs)
    x_rows = jnp.einsum(
        "pc,tc->pt",
        order,
        jnp.concatenate([x_mine, x_theirs]),
        preferred_element_type=F32,
    ).astype(BF)
    x_other = swapped(x_rows[channels // 2 :], "seq", 1)
    x_rows = x_rows[: channels // 2]
    weights_got = after(weights_got, x_other)
    weights_other = swapped(weights_got, "seq", 1)
    cot_other = swapped(cot_window, "seq", 1)
    half_rows = channels // 2
    n = 2 * half
    send_first, att_first, back_attended, scale_first = attention_call(
        first_kernel,
        "first_heads",
        group,
        head_dim,
        ((3 * group, n), (group, n), (channels, n)),
        (nums, head_scale, x_mine, x_theirs, cot_window, w_qkv, w_proj, weights_got, weights_other),
        24,
    )
    got_first = swapped(send_first, "seq", 1)
    own, *sends = chip_gradient(group, (x_rows, x_other, send_first, got_first))
    rest = channels - group
    send_second, att_rows, back_mine, window_send, att_mine, scale_second = attention_call(
        second_kernel,
        "second_heads",
        rest,
        head_dim,
        (
            (3 * rest + half_rows, n),
            (half_rows, n),
            (half, channels),
            (n, channels),
            (half, channels),
        ),
        (
            nums,
            head_scale,
            x_mine,
            x_theirs,
            order,
            after(back_attended, own),
            att_first,
            send_first,
            w_qkv,
            weights_got,
            weights_other,
        ),
        60,
        (rest,),
    )
    first_own, first_sends = own, sends
    got_second = swapped(send_second, "seq", 1)
    first_total = sum_square(first_own, first_sends, place)
    own, *sends = chip_gradient(
        rest,
        (
            after(x_rows, back_mine, first_total),
            x_other,
            send_second,
            got_second,
            att_rows,
            cot_window,
            cot_other,
        )
    )
    window_got = after(window_partner(window_send), own)
    back_mixed, inner, outer, output, small = field_back(
        (
            nums,
            back_mine,
            att_mine,
            window_got,
            mixed_field,
            cot,
            tokens,
            before,
            behind,
            norm_gain,
            scale_first,
            scale_second,
            w_proj,
            weights_got,
            weights_other,
        )
    )
    second_total = sum_square(after(own, small), sends, place)
    first_block = sum_chips(first_total, place, second_total)
    hold = []
    steps = sum_steps(after(small, second_total), place, hold)
    small = next(steps)
    small = next(steps)
    second_block = sum_chips(second_total, place)
    small = next(steps)
    factor = 1.0 / math.sqrt(
        lax.axis_size("rep") * lax.axis_size("dp") * lax.axis_size("seq") * positions
    )
    first_parts = gather_blocks(first_block, place)
    second_parts = gather_blocks(second_block, place, small)
    hold.append(second_parts[0])
    grad_qkv, grad_proj = assemble(nums, first_parts, second_parts, place, factor, group)
    inner = swapped(after(inner, second_total), "seq", 1)
    outer = edge_partner(after(outer, second_total))
    low = core == 0
    grad_tokens = field_gradient(
        (back_mixed, jnp.where(low, outer, inner), jnp.where(low, inner, outer), conv_weight)
    )
    for small in steps:
        pass
    small = small * factor
    taps = conv_weight.shape[0]
    return (
        output[None],
        grad_tokens[None],
        grad_qkv,
        grad_proj,
        small[:taps],
        small[taps],
        small[taps + 1, :head_count],
    )


def solution(mesh):
    block = P(("rep", "dp"), "seq", None, None, None)
    rows = P("dp", None)
    return jax.shard_map(
        per_device,
        mesh=mesh,
        in_specs=(block, block, rows, rows, P(), P(), P(), P()),
        out_specs=(block, block, rows, rows, P(), P(), P()),
        check_vma=False,
    )
```
